256 devices in a mesh: seq: 32 (over y_hi, z, core), chan: 8 (over y_lo, x).
Axes of the slice: x: 4, y: 4 (y_hi: 2, y_lo: 2; y = y_hi * 2 + y_lo), z: 8, core: 2. Of those that a mesh axis runs over, the one named last changes fastest.
Arguments:
- tokens: bfloat16 [65536, 2048], P('seq', 'chan'), may hold values from -6 to 6
- spectrum: bfloat16 [2, 256, 512, 2048], P(None, 'seq', None, 'chan'), may hold values from -6 to 6
- skip_gain: float32 [2048], P('chan'), may hold values from -1 to 1
- norm_gain: float32 [2048], P('chan'), may hold values from 0.1 to 1.9
- gate_first: bfloat16 [8, 256, 256], P('chan'), may hold values from -0.375 to 0.375
- up_first: bfloat16 [8, 256, 256], P('chan'), may hold values from -0.375 to 0.375
- gate_second: bfloat16 [8, 256, 1024], P('chan'), may hold values from -0.375 to 0.375
- up_second: bfloat16 [8, 256, 1024], P('chan'), may hold values from -0.375 to 0.375
- down_first: bfloat16 [8, 1024, 256], P('chan'), may hold values from -0.1875 to 0.1875
- down_second: bfloat16 [8, 256, 256], P('chan'), may hold values from -0.375 to 0.375
Outputs:
- layer_out: bfloat16 [65536, 2048], P('seq', 'chan')
The draws below stay inside these ranges and needn't reach their ends.
All inputs are finite; a program needn't handle non-finite values.
Results may differ from the reference program's by a relative error of at most 0.017.
Values may be sent and summed in bfloat16 or wider, within the bound.
No kernel may reach another device: no remote copies, remote signals or barrier semaphores. Data moves between devices by JAX's collectives and lax.ppermute only.
A program may use at most 128 MiB of HBM per device.

```python
import math
import jax
import jax.numpy as jnp
from jax import lax

D = 2048
COLS = 512
BLOCKS = 8
PB = 256
HB = 1024
PIECE = 32
ROWS = 128
AROWS = 256
TOKENS = 65536
SPAN = 131072


def shard_levels(own_key, dims, shards, smallest, high):
    def one(axis_at, parts):
        heights = jax.random.uniform(jax.random.fold_in(jax.random.fold_in(own_key, 6), axis_at), (parts,), jnp.float32, smallest / len(shards), high / len(shards))
        return jnp.repeat(jnp.exp(heights), dims[axis_at] // parts).reshape((-1,) + (1,) * (len(dims) - axis_at - 1))

    factor_of = one(*shards[0])
    for cut in shards[1:]:
        factor_of = factor_of * one(*cut)
    return factor_of


def scatter_about(stream_key, dims, spread, bound, split=(), dtype=jnp.bfloat16):
    entries = spread * jax.random.normal(stream_key, dims, jnp.float32)
    if split:
        entries = entries * shard_levels(stream_key, dims, split, -0.22, 0.18)
    return jnp.clip(entries, -bound, bound).astype(dtype)


def setup_inputs(seed: int = 0) -> dict:
    streams_of = jax.random.split(jax.random.key(seed), 11)
    return {
        "tokens": scatter_about(streams_of[0], (TOKENS, D), 1.0, 6.0, ((0, 32), (1, 8))),
        "spectrum": scatter_about(streams_of[1], (2, AROWS, COLS, D), 1.0, 6.0, ((1, 32), (3, 8))),
        "skip_gain": jnp.clip(jax.random.uniform(streams_of[2], (D,), jnp.float32, -1.0, 1.0) * shard_levels(streams_of[2], (D,), ((0, 8),), -0.4, 0.0), -1.0, 1.0),
        "norm_gain": jnp.clip(1.0 + 0.18 * jax.random.normal(streams_of[3], (D,), jnp.float32), 0.1, 1.9),
        "gate_first": scatter_about(streams_of[4], (BLOCKS, PB, PB), PB ** -0.5, 0.375, ((0, 8),)),
        "up_first": scatter_about(streams_of[5], (BLOCKS, PB, PB), PB ** -0.5, 0.375, ((0, 8),)),
        "gate_second": scatter_about(streams_of[6], (BLOCKS, PB, HB), PB ** -0.5, 0.375, ((0, 8),)),
        "up_second": scatter_about(streams_of[7], (BLOCKS, PB, HB), PB ** -0.5, 0.375, ((0, 8),)),
        "down_first": scatter_about(streams_of[8], (BLOCKS, HB, PB), HB ** -0.5, 0.1875, ((0, 8),)),
        "down_second": scatter_about(streams_of[9], (BLOCKS, PB, PB), PB ** -0.5, 0.375, ((0, 8),)),
    }


def row_table(total_rows, real_rows):
    crow = lax.broadcasted_iota(jnp.int32, (total_rows, real_rows), 0)
    arow = lax.broadcasted_iota(jnp.int32, (total_rows, real_rows), 1)
    angles = 2.0 * math.pi / total_rows * (crow * arow % total_rows).astype(jnp.float32)
    return jnp.stack([jnp.cos(angles), -jnp.sin(angles)]).astype(jnp.bfloat16)

def column_tables(width):
    first = lax.broadcasted_iota(jnp.int32, (width, width), 0)
    second = lax.broadcasted_iota(jnp.int32, (width, width), 1)
    angles = 2.0 * math.pi / width * (first * second % width).astype(jnp.float32)
    cosine = jnp.cos(angles)
    sine = jnp.sin(angles)
    forward = jnp.stack([jnp.stack([cosine, -sine]), jnp.stack([sine, cosine])]).astype(jnp.bfloat16)
    inverse = jnp.stack([jnp.stack([cosine, sine]), jnp.stack([-sine, cosine])]).astype(jnp.bfloat16)
    return (forward, inverse)

def twiddle(row_start, rows, col_start, cols, span):
    crow = row_start + lax.broadcasted_iota(jnp.int32, (rows, cols), 0)
    bcol = col_start + lax.broadcasted_iota(jnp.int32, (rows, cols), 1)
    angles = 2.0 * math.pi / span * (crow * bcol % span).astype(jnp.float32)
    return (jnp.cos(angles)[:, :, None], jnp.sin(angles)[:, :, None])

def forward_rows(block, col_start, span):
    real_rows, width = (block.shape[0], block.shape[1])
    table = row_table(2 * real_rows, real_rows).astype(jnp.float32)
    spectra = jnp.einsum('kca,abh->kcbh', table, block.astype(jnp.float32))
    cosine, sine = twiddle(0, 2 * real_rows, col_start, width, span)
    real_part = spectra[0] * cosine + spectra[1] * sine
    imag_part = spectra[1] * cosine - spectra[0] * sine
    return jnp.stack([real_part, imag_part]).astype(jnp.bfloat16)

def middle_part(freq, kernel, row_start, span):
    rows, width = (freq.shape[1], freq.shape[2])
    forward, inverse = column_tables(width)
    spectra = jnp.einsum('kcbh,kjbd->jcdh', freq.astype(jnp.float32), forward.astype(jnp.float32))
    kernel_f = kernel.astype(jnp.float32)
    prod_real = spectra[0] * kernel_f[0] - spectra[1] * kernel_f[1]
    prod_imag = spectra[0] * kernel_f[1] + spectra[1] * kernel_f[0]
    product = jnp.stack([prod_real, prod_imag]).astype(jnp.bfloat16)
    back = jnp.einsum('kcdh,kjdb->jcbh', product.astype(jnp.float32), inverse.astype(jnp.float32))
    cosine, sine = twiddle(row_start, rows, 0, width, span)
    real_part = back[0] * cosine - back[1] * sine
    imag_part = back[1] * cosine + back[0] * sine
    return jnp.stack([real_part, imag_part]).astype(jnp.bfloat16)

def final_rows(freq, span):
    total_rows = freq.shape[1]
    table = row_table(total_rows, total_rows // 2).astype(jnp.float32)
    summed = jnp.einsum('kcbh,kca->abh', freq.astype(jnp.float32), table)
    return (summed * (1.0 / span)).astype(jnp.bfloat16)

def mlp_block(stream_rows, norm_gain, gate_first, up_first, gate_second, up_second, down_first, down_second):
    count = stream_rows.shape[0]
    stream_f = stream_rows.astype(jnp.float32)
    meansq = lax.optimization_barrier(jnp.sum(stream_f * stream_f, axis=1)) / D
    normed = (stream_f * lax.rsqrt(meansq + 1e-05)[:, None] * norm_gain).astype(jnp.bfloat16)
    normed = normed.reshape(count, BLOCKS, PB).astype(jnp.float32)
    gate_mid = jnp.einsum('tip,ipq->tiq', normed, gate_first.astype(jnp.float32)).astype(jnp.bfloat16)
    up_mid = jnp.einsum('tip,ipq->tiq', normed, up_first.astype(jnp.float32)).astype(jnp.bfloat16)
    gate_mid = gate_mid.reshape(count, BLOCKS, BLOCKS, PIECE).astype(jnp.float32)
    up_mid = up_mid.reshape(count, BLOCKS, BLOCKS, PIECE).astype(jnp.float32)
    gate_w = gate_second.reshape(BLOCKS, BLOCKS, PIECE, HB).astype(jnp.float32)
    up_w = up_second.reshape(BLOCKS, BLOCKS, PIECE, HB).astype(jnp.float32)
    gate = jnp.einsum('tijm,jimh->tjh', gate_mid, gate_w)
    upper = jnp.einsum('tijm,jimh->tjh', up_mid, up_w)
    act = (jax.nn.gelu(gate, approximate=True) * upper).astype(jnp.bfloat16)
    down_mid = jnp.einsum('tjh,jhq->tjq', act.astype(jnp.float32), down_first.astype(jnp.float32)).astype(jnp.bfloat16)
    down_mid = down_mid.reshape(count, BLOCKS, BLOCKS, PIECE).astype(jnp.float32)
    down_w = down_second.reshape(BLOCKS, BLOCKS, PIECE, PB).astype(jnp.float32)
    result = jnp.einsum('tjom,ojmp->top', down_mid, down_w).reshape(count, D)
    return (stream_f + result).astype(jnp.bfloat16)

def reference(tokens, spectrum, skip_gain, norm_gain, gate_first, up_first, gate_second, up_second, down_first, down_second):
    grid = tokens.reshape(ROWS, COLS, D)
    width_chan = D // 8
    results = []
    for block_index in range(8):
        lower = block_index * width_chan
        part = grid[:, :, lower:lower + width_chan]
        freq = forward_rows(part, 0, SPAN)
        mixed = middle_part(freq, spectrum[:, :, :, lower:lower + width_chan], 0, SPAN)
        results.append(final_rows(mixed, SPAN))
    conv = jnp.concatenate(results, axis=2).reshape(TOKENS, D)
    stream = (conv.astype(jnp.float32) + skip_gain * tokens.astype(jnp.float32)).astype(jnp.bfloat16)
    row_block = min(TOKENS, 4096)
    stacked = stream.reshape(TOKENS // row_block, row_block, D)

    def apply_block(rows_in):
        return mlp_block(rows_in, norm_gain, gate_first, up_first, gate_second, up_second, down_first, down_second)
    return lax.map(apply_block, stacked).reshape(TOKENS, D)
```

```python
import functools

import jax
import jax.numpy as jnp
import ml_dtypes
import numpy as np
from jax import lax
from jax.experimental import pallas as pl
from jax.experimental.pallas import tpu as pltpu
from jax.sharding import PartitionSpec as P

D = 2048
COLS = 512
AROWS = 256
SPAN = 131072
SEQ = 32
CHAN = 8
OWN = 8
WIDTH = 256
PB = 256
HB = 1024
PIECE = 32
ROWS_DEV = 4
S_ROWS = 128
X_ROWS = 32
F32 = jnp.float32
BF16 = jnp.bfloat16
VMEM_LIMIT = 56 * 1024 * 1024


def bf16(values):
    return np.asarray(values, np.float64).astype(np.float32).astype(ml_dtypes.bfloat16)


def angle(product, period):
    return 2.0 * np.pi / period * (product % period)


@functools.lru_cache(None)
def tables():
    cols = np.arange(COLS)
    perm_cols = (cols % 128) * 4 + cols // 128
    perm = np.zeros((COLS, COLS))
    perm[cols, perm_cols] = 1.0
    c = np.arange(AROWS)
    rows = angle(c[:, None] * np.arange(AROWS // 2)[None, :], AROWS)
    row_fwd = np.concatenate([np.cos(rows), -np.sin(rows)], 0)
    row_inv = row_fwd.T
    theta = angle(c[:, None] * perm_cols[None, :], SPAN)
    fwd, inv = [], []
    for q in range(4):
        ang = angle((4 * np.arange(128) + q)[:, None] * np.arange(128)[None, :], COLS)
        co, si = np.cos(ang), np.sin(ang)
        fwd.append(np.block([[co, -si], [si, co]]))
        inv.append(np.block([[co.T, si.T], [-si.T, co.T]]))
    return dict(
        perm=bf16(perm),
        eye=bf16(np.eye(WIDTH)),
        row_fwd=bf16(row_fwd),
        row_inv=bf16(row_inv),
        cos=np.cos(theta).astype(np.float32),
        sin=np.sin(theta).astype(np.float32),
        fwd=bf16(np.stack(fwd)),
        inv=bf16(np.stack(inv)),
    )


def dot(a, b):
    return jnp.dot(a, b, preferred_element_type=F32)


def dot_nt(a, b):
    return lax.dot_general(a, b, (((1,), (1,)), ((), ())), preferred_element_type=F32)


def params():
    return pltpu.CompilerParams(vmem_limit_bytes=VMEM_LIMIT)


def pack_kernel(tok_ref, spec_ref, eye_ref, perm_ref, msg_ref, xt_ref):
    step = pl.program_id(0)
    eye = eye_ref[...]

    def turned(tile):
        return dot_nt(eye, tile).reshape(SEQ, OWN, COLS)

    @pl.when(step < 8)
    def _():
        msg_ref[...] = jnp.concatenate([turned(spec_ref[0]), turned(spec_ref[1])], 1).astype(BF16)

    @pl.when(step >= 8)
    def _():
        perm = perm_ref[...]
        first = dot(perm, tok_ref[0]).astype(BF16)
        second = dot(perm, tok_ref[1]).astype(BF16)
        both = jnp.concatenate([turned(first), turned(second)], 1).astype(BF16)
        msg_ref[...] = both
        xt_ref[...] = both


def pack(tokens, spectrum, tb):
    tok = tokens.reshape(ROWS_DEV, COLS, WIDTH)
    spec = spectrum.reshape(16, COLS, WIDTH)
    return pl.pallas_call(
        pack_kernel,
        grid=(10,),
        in_specs=[
            pl.BlockSpec((2, COLS, WIDTH), lambda g: (jnp.maximum(g - 8, 0), 0, 0)),
            pl.BlockSpec((2, COLS, WIDTH), lambda g: (jnp.minimum(g, 7), 0, 0)),
            pl.BlockSpec((WIDTH, WIDTH), lambda g: (0, 0)),
            pl.BlockSpec((COLS, COLS), lambda g: (0, 0)),
        ],
        out_specs=[
            pl.BlockSpec((SEQ, 16, COLS), lambda g: (0, g, 0)),
            pl.BlockSpec((SEQ, 16, COLS), lambda g: (0, jnp.maximum(g - 8, 0), 0)),
        ],
        out_shape=[
            jax.ShapeDtypeStruct((SEQ, S_ROWS + X_ROWS, COLS), BF16),
            jax.ShapeDtypeStruct((SEQ, X_ROWS, COLS), BF16),
        ],
        compiler_params=params(),
        name="pack",
    )(tok, spec, tb["eye"], tb["perm"])


CH_C = 64
CH_S = 8
CH_M = CH_C * OWN


def conv_kernel(
    spec_ref, x_ref, row_fwd_ref, row_inv_ref, cos_ref, sin_ref, fwd_ref, inv_ref,
    out_ref, rows_f, y_s, x4_s, spec_f, p_s, v_s,
):
    step = pl.program_id(0)

    @pl.when(step == 0)
    def _():
        for q in range(4):
            x_q = x_ref[:, :, q * 128 : q * 128 + 128]
            rows_f[q] = x_q.reshape(AROWS // 2 * OWN, 128).astype(F32)

        @pl.loop(0, OWN)
        def _(h):
            every = pl.ds(h, AROWS // 2, stride=OWN)
            x_h = jnp.concatenate([rows_f[q, every, :] for q in range(4)], 1).astype(BF16)
            for half in range(2):
                c0 = half * 128
                f0 = dot(row_fwd_ref[pl.ds(c0, 128), :], x_h)
                f1 = dot(row_fwd_ref[pl.ds(AROWS + c0, 128), :], x_h)
                co, si = cos_ref[pl.ds(c0, 128), :], sin_ref[pl.ds(c0, 128), :]
                y0 = (f0 * co + f1 * si).astype(BF16)
                y1 = (f1 * co - f0 * si).astype(BF16)
                for q in range(4):
                    y_s[h, pl.ds(c0, 128), pl.ds(q * 256, 128)] = y0[:, q * 128 : q * 128 + 128]
                    y_s[h, pl.ds(c0, 128), pl.ds(q * 256 + 128, 128)] = y1[:, q * 128 : q * 128 + 128]

    c_start = pl.multiple_of(step * CH_C, CH_C)
    for k in range(2):
        for r in range(4):
            part = spec_ref[:, k * 64 : k * 64 + 64, r * 128 : r * 128 + 128]
            spec_f[k, r] = part.reshape(CH_M, 128).astype(F32)
    for q in range(4):
        part = y_s[:, pl.ds(c_start, CH_C), q * 256 : q * 256 + 256].reshape(CH_M, 256)
        x4_s[q] = dot(part, fwd_ref[q])

    @pl.loop(0, OWN)
    def _(h):
        for rb in range(CH_C // 16):
            r0 = pl.multiple_of(h * CH_C + rb * 16, 16)
            rows = pl.ds(r0, 16)
            srows = pl.ds(h + rb * 16 * OWN, 16, stride=OWN)
            re = [x4_s[q, rows, 0:128] for q in range(4)]
            im = [x4_s[q, rows, 128:256] for q in range(4)]
            t0r, t0i = re[0] + re[2], im[0] + im[2]
            t1r, t1i = re[0] - re[2], im[0] - im[2]
            t2r, t2i = re[1] + re[3], im[1] + im[3]
            t3r, t3i = re[1] - re[3], im[1] - im[3]
            zr = [t0r + t2r, t1r + t3i, t0r - t2r, t1r - t3i]
            zi = [t0i + t2i, t1i - t3r, t0i - t2i, t1i + t3r]
            pr, pi = [], []
            for r in range(4):
                sr = spec_f[0, r, srows, :]
                si = spec_f[1, r, srows, :]
                pr.append(zr[r] * sr - zi[r] * si)
                pi.append(zr[r] * si + zi[r] * sr)
            u0r, u0i = pr[0] + pr[2], pi[0] + pi[2]
            u1r, u1i = pr[0] - pr[2], pi[0] - pi[2]
            u2r, u2i = pr[1] + pr[3], pi[1] + pi[3]
            u3r, u3i = pr[1] - pr[3], pi[1] - pi[3]
            qr = [u0r + u2r, u1r - u3i, u0r - u2r, u1r + u3i]
            qi = [u0i + u2i, u1i + u3r, u0i - u2i, u1i - u3r]
            for q in range(4):
                p_s[rows, q * 256 : q * 256 + 128] = qr[q].astype(BF16)
                p_s[rows, q * 256 + 128 : q * 256 + 256] = qi[q].astype(BF16)

    for q in range(4):
        x4_s[q] = dot(p_s[:, q * 256 : q * 256 + 256], inv_ref[q])

    @pl.loop(0, OWN)
    def _(h):
        rows = pl.ds(pl.multiple_of(h * CH_C, CH_C), CH_C)
        crow = pl.ds(c_start, CH_C)
        for q in range(4):
            lanes = slice(q * 128, q * 128 + 128)
            co, si = cos_ref[crow, lanes], sin_ref[crow, lanes]
            q0, q1 = x4_s[q, rows, 0:128], x4_s[q, rows, 128:256]
            v_s[h, crow, lanes] = (q0 * co - q1 * si).astype(BF16)
            v_s[h, pl.ds(AROWS + c_start, CH_C), lanes] = (q1 * co + q0 * si).astype(BF16)

    @pl.when(step == pl.num_programs(0) - 1)
    def _():
        @pl.loop(0, OWN)
        def _(h):
            every = pl.ds(h, AROWS // 2, stride=OWN)
            rows = dot(row_inv_ref[...], v_s[h]) * (1.0 / SPAN)
            for q in range(4):
                rows_f[q, every, :] = rows[:, q * 128 : q * 128 + 128]

        for q in range(4):
            part = rows_f[q].astype(BF16).reshape(SEQ, X_ROWS, 128)
            out_ref[:, :, q * 128 : q * 128 + 128] = part


def convolve(msg, tb):
    whole = lambda *shape: pl.BlockSpec(shape, lambda g: (0,) * len(shape))
    return pl.pallas_call(
        conv_kernel,
        grid=(AROWS // CH_C,),
        in_specs=[
            pl.BlockSpec((CH_S, S_ROWS, COLS), lambda g: (g, 0, 0)),
            pl.BlockSpec((SEQ, X_ROWS, COLS), lambda g: (0, S_ROWS // X_ROWS, 0)),
            whole(2 * AROWS, AROWS // 2),
            whole(AROWS // 2, 2 * AROWS),
            whole(AROWS, COLS),
            whole(AROWS, COLS),
            whole(4, 256, 256),
            whole(4, 256, 256),
        ],
        out_specs=whole(SEQ, X_ROWS, COLS),
        out_shape=jax.ShapeDtypeStruct((SEQ, X_ROWS, COLS), BF16),
        scratch_shapes=[
            pltpu.VMEM((4, AROWS // 2 * OWN, 128), F32),
            pltpu.VMEM((OWN, AROWS, 2 * COLS), BF16),
            pltpu.VMEM((4, CH_M, 256), F32),
            pltpu.VMEM((2, 4, CH_M, 128), F32),
            pltpu.VMEM((CH_M, 2 * COLS), BF16),
            pltpu.VMEM((OWN, 2 * AROWS, COLS), BF16),
        ],
        compiler_params=params(),
        name="convolve",
    )(msg, msg, tb["row_fwd"], tb["row_inv"], tb["cos"], tb["sin"], tb["fwd"], tb["inv"])


G_ROWS = 4 * 2 * PIECE + 16


def first_kernel(conv_ref, xt_ref, skip_ref, gain_ref, w_ref, out_ref, stream_ref):
    skip, gain = skip_ref[...], gain_ref[...]
    w = w_ref[...]
    sums = []
    for pair in range(2):
        rows = slice(pair * 16, pair * 16 + 16)
        conv = conv_ref[:, rows, :].astype(F32)
        xt = xt_ref[:, rows, :].astype(F32)
        kept = []
        for sub in range(2):
            tc = pair * 2 + sub
            part = slice(sub * 8, sub * 8 + 8)
            stream = (conv[:, part, :] + skip * xt[:, part, :]).astype(BF16).astype(F32)
            kept.append(stream)
            sums.append(jnp.sum(jnp.sum(stream * stream, axis=0), axis=0, keepdims=True))
            scaled = (stream * gain).reshape(WIDTH, COLS).astype(BF16)
            mid = dot(w, scaled).astype(BF16)
            for j in range(CHAN):
                r0 = tc * 2 * PIECE
                out_ref[j, r0 : r0 + PIECE, :] = mid[j * PIECE : (j + 1) * PIECE]
                out_ref[j, r0 + PIECE : r0 + 2 * PIECE, :] = mid[PB + j * PIECE : PB + (j + 1) * PIECE]
        stream_ref[:, rows, :] = jnp.concatenate(kept, 1).astype(BF16)
    total = jnp.concatenate(sums, 0)
    high = total.astype(BF16).astype(F32)
    tail = jnp.concatenate([high, total - high, jnp.zeros((8, COLS), F32)], 0).astype(BF16)
    for j in range(CHAN):
        out_ref[j, 4 * 2 * PIECE :, :] = tail


def first(conv, xt, skip, gain, w):
    return pl.pallas_call(
        first_kernel,
        out_shape=[
            jax.ShapeDtypeStruct((CHAN, G_ROWS, COLS), BF16),
            jax.ShapeDtypeStruct((SEQ, X_ROWS, COLS), BF16),
        ],
        compiler_params=params(),
        name="first",
    )(conv, xt, skip, gain, w)


def second_kernel(mid_ref, sum_ref, gate_ref, up_ref, down_ref, out_ref):
    step = pl.program_id(0)
    total = jnp.sum(sum_ref[...].astype(F32), axis=0)
    pick = lax.broadcasted_iota(jnp.int32, (16, 1), 0)
    mine = jnp.logical_or(pick == step, pick == step + 4)
    total = jnp.sum(jnp.where(mine, total, 0.0), axis=0, keepdims=True)
    scale = lax.rsqrt(total * (1.0 / D) + 1e-05)
    gate_in = mid_ref[:, 0:PIECE, :].reshape(PB, COLS)
    up_in = mid_ref[:, PIECE : 2 * PIECE, :].reshape(PB, COLS)
    acc = jnp.zeros((PB, COLS), F32)
    for e in range(4):
        rows = slice(e * 256, e * 256 + 256)
        gate = dot(gate_ref[rows, :], gate_in) * scale
        upper = dot(up_ref[rows, :], up_in) * scale
        act = (jax.nn.gelu(gate, approximate=True) * upper).astype(BF16)
        acc = acc + dot(down_ref[:, rows], act)
    out_ref[...] = acc.astype(BF16).reshape(CHAN, PIECE, COLS)


def second(mid, gate_w, up_w, down_w):
    whole = lambda *shape: pl.BlockSpec(shape, lambda g: (0,) * len(shape))
    return pl.pallas_call(
        second_kernel,
        grid=(ROWS_DEV,),
        in_specs=[
            pl.BlockSpec((CHAN, 2 * PIECE, COLS), lambda g: (0, g, 0)),
            pl.BlockSpec((CHAN, 16, COLS), lambda g: (0, 4 * 2 * PIECE // 16, 0)),
            whole(HB, PB),
            whole(HB, PB),
            whole(PB, HB),
        ],
        out_specs=pl.BlockSpec((CHAN, PIECE, COLS), lambda g: (0, g, 0)),
        out_shape=jax.ShapeDtypeStruct((CHAN, ROWS_DEV * PIECE, COLS), BF16),
        compiler_params=params(),
        name="second",
    )(mid, mid, gate_w, up_w, down_w)


def last_kernel(down_ref, stream_ref, w_ref, perm_ref, out_ref):
    w, perm = w_ref[...], perm_ref[...]
    stream = stream_ref[...].astype(F32)
    for sub in range(2):
        down = down_ref[:, sub * PIECE : (sub + 1) * PIECE, :].reshape(PB, COLS)
        kept = stream[:, sub * 8 : sub * 8 + 8, :].reshape(WIDTH, COLS)
        res = (kept + dot(w, down)).astype(BF16)
        out_ref[sub * COLS : (sub + 1) * COLS, :] = dot_nt(perm, res).astype(BF16)


def last(down, stream, w, tb):
    whole = lambda *shape: pl.BlockSpec(shape, lambda g: (0,) * len(shape))
    return pl.pallas_call(
        last_kernel,
        grid=(2,),
        in_specs=[
            pl.BlockSpec((CHAN, 2 * PIECE, COLS), lambda g: (0, g, 0)),
            pl.BlockSpec((SEQ, 16, COLS), lambda g: (0, g, 0)),
            whole(PB, PB),
            whole(COLS, COLS),
        ],
        out_specs=pl.BlockSpec((2 * COLS, WIDTH), lambda g: (g, 0)),
        out_shape=jax.ShapeDtypeStruct((ROWS_DEV * COLS, WIDTH), BF16),
        compiler_params=params(),
        name="last",
    )(down, stream, w, np.ascontiguousarray(tb["perm"].T))


def exchange(value, axis):
    return lax.all_to_all(value, axis, split_axis=0, concat_axis=0, tiled=True)


def per_device(
    tokens, spectrum, skip_gain, norm_gain,
    gate_first, up_first, gate_second, up_second, down_first, down_second,
):
    tb = tables()
    msg, xt = pack(tokens, spectrum, tb)
    conv = convolve(exchange(msg, "seq"), tb)
    conv = exchange(conv, "seq")
    first_w = jnp.concatenate([gate_first[0].T, up_first[0].T], 0)
    skip = skip_gain.reshape(SEQ, OWN, 1)
    gain = norm_gain.reshape(SEQ, OWN, 1)
    mid, stream = first(conv, xt, skip, gain, first_w)
    down = second(exchange(mid, "chan"), gate_second[0].T, up_second[0].T, down_first[0].T)
    return last(exchange(down, "chan"), stream, down_second[0].T, tb)


def solution(mesh):
    in_specs = (
        P("seq", "chan"),
        P(None, "seq", None, "chan"),
        P("chan"),
        P("chan"),
        P("chan", None, None),
        P("chan", None, None),
        P("chan", None, None),
        P("chan", None, None),
        P("chan", None, None),
        P("chan", None, None),
    )
    return jax.shard_map(
        per_device, mesh=mesh, in_specs=in_specs, out_specs=P("seq", "chan"), check_vma=False
    )
```

```python
import functools

import jax
import jax.numpy as jnp
import ml_dtypes
import numpy as np
from jax import lax
from jax.experimental import pallas as pl
from jax.experimental.pallas import tpu as pltpu
from jax.sharding import PartitionSpec as P

D = 2048
COLS = 512
AROWS = 256
SPAN = 131072
SEQ = 32
CHAN = 8
OWN = 8
WIDTH = 256
PB = 256
HB = 1024
PIECE = 32
ROWS_DEV = 4
TOK = 256
S_ROWS = 128
X_ROWS = 32
F32 = jnp.float32
BF16 = jnp.bfloat16
VMEM_LIMIT = 56 * 1024 * 1024


def bf16(values):
    return np.asarray(values, np.float64).astype(np.float32).astype(ml_dtypes.bfloat16)


def angle(product, period):
    return 2.0 * np.pi / period * (product % period)


@functools.lru_cache(None)
def tables():
    cols = np.arange(COLS)
    perm_cols = (cols % 128) * 4 + cols // 128
    perm = np.zeros((COLS, COLS))
    perm[cols, perm_cols] = 1.0
    place = np.arange(TOK)
    token = 4 * (place % 64) + 2 * (place // 128) + place // 64 % 2
    unperm = np.zeros((TOK, TOK))
    unperm[token, place] = 1.0
    c = np.arange(AROWS)
    rows = angle(c[:, None] * np.arange(AROWS // 2)[None, :], AROWS)
    row_fwd = np.concatenate([np.cos(rows), -np.sin(rows)], 0)
    row_inv = row_fwd.T
    theta = angle(c[:, None] * perm_cols[None, :], SPAN)
    fwd, inv = [], []
    for q in range(4):
        ang = angle((4 * np.arange(128) + q)[:, None] * np.arange(128)[None, :], COLS)
        co, si = np.cos(ang), np.sin(ang)
        fwd.append(np.block([[co, -si], [si, co]]))
        inv.append(np.block([[co.T, si.T], [-si.T, co.T]]))
    return dict(
        perm=bf16(perm),
        unperm=bf16(unperm),
        row_fwd=bf16(row_fwd),
        row_inv=bf16(row_inv),
        cos=np.cos(theta).astype(np.float32),
        sin=np.sin(theta).astype(np.float32),
        fwd=bf16(np.stack(fwd)),
        inv=bf16(np.stack(inv)),
    )


def dot(a, b):
    return jnp.dot(a, b, preferred_element_type=F32)


def dot_nt(a, b):
    return lax.dot_general(a, b, (((1,), (1,)), ((), ())), preferred_element_type=F32)


def params():
    return pltpu.CompilerParams(vmem_limit_bytes=VMEM_LIMIT)


W_ROWS = 1936
PIECES = 4


def turn_weights(g1_ref, u1_ref, g2_ref, u2_ref, d1_ref, d2_ref, gain_ref, out_ref):
    tiles = [g2_ref[0, :, 0:256], g2_ref[0, :, 256:512], u2_ref[0, :, 0:256], u2_ref[0, :, 256:512]]
    tiles += [d1_ref[0, 0:256, :], d1_ref[0, 256:512, :]]
    for n, tile in enumerate(tiles):
        out_ref[n * 256 : n * 256 + 256, :] = tile.T
    for n, ref in enumerate((g1_ref, u1_ref, d2_ref)):
        r0 = 1536 + n * 128
        out_ref[r0 : r0 + 128, :] = ref[0].T
    gain = gain_ref[...]
    high = gain.astype(BF16).astype(F32)
    mid = (gain - high).astype(BF16).astype(F32)
    low = gain - high - mid
    out_ref[1920:, :] = jnp.concatenate([high, mid, low, jnp.zeros((13, PB), F32)], 0).astype(BF16)


def pack_kernel(core_ref, tok_ref, spec_ref, perm_ref, *refs):
    weight_refs, (msg_ref, w_ref, msg_s, w_s, msg_sem, w_sem) = refs[:7], refs[7:]
    step = pl.program_id(0)

    def turned(tiles):
        tiles = [tile.T.astype(F32).reshape(SEQ, OWN, COLS) for tile in tiles]
        return jnp.concatenate(tiles, 1).astype(BF16)

    def copies(at):
        rows = pl.ds(pl.multiple_of(at * 32, 32), 32)
        for n in range(PIECES):
            part = pl.ds(n * (SEQ // PIECES), SEQ // PIECES)
            yield pltpu.make_async_copy(
                msg_s.at[part, rows, :], msg_ref.at[part, rows, :], msg_sem.at[at, n]
            )

    w_copy = pltpu.make_async_copy(w_s, w_ref, w_sem)

    @pl.when(step < 4)
    def _():
        for n in range(2):
            rows = pl.ds(pl.multiple_of(step * 32 + n * 16, 16), 16)
            msg_s[:, rows, :] = turned([spec_ref[2 * n], spec_ref[2 * n + 1]])

    @pl.when(step == 4)
    def _():
        perm = perm_ref[...]
        for n in range(2):
            tiles = [dot(perm, tok_ref[2 * n + m]).astype(BF16) for m in range(2)]
            msg_s[:, S_ROWS + n * 16 : S_ROWS + n * 16 + 16, :] = turned(tiles)

    for copy in copies(step):
        copy.start()

    @pl.when(step == 1)
    def _():
        turn_weights(*weight_refs, w_s)
        w_copy.start()

    @pl.when(step == 4)
    def _():
        for at in range(5):
            for copy in copies(at):
                copy.wait()
        w_copy.wait()


def pack(tokens, spectrum, core, weights, gain, tb):
    tok = tokens.reshape(ROWS_DEV, COLS, WIDTH)
    spec = spectrum.reshape(16, COLS, WIDTH)
    whole = lambda *shape: pl.BlockSpec(shape, lambda g, core: (0,) * len(shape))
    cols = lambda n: pl.BlockSpec((1, PB, n), lambda g, core: (0, 0, core[0]))
    hbm = pl.BlockSpec(memory_space=pltpu.HBM)
    return pl.pallas_call(
        pack_kernel,
        grid_spec=pltpu.PrefetchScalarGridSpec(
            num_scalar_prefetch=1,
            grid=(5,),
            in_specs=[
                whole(ROWS_DEV, COLS, WIDTH),
                pl.BlockSpec((4, COLS, WIDTH), lambda g, core: (jnp.minimum(g, 3), 0, 0)),
                whole(COLS, COLS),
                cols(128),
                cols(128),
                cols(512),
                cols(512),
                pl.BlockSpec((1, 512, PB), lambda g, core: (0, core[0], 0)),
                cols(128),
                whole(1, WIDTH),
            ],
            out_specs=[hbm, hbm],
            scratch_shapes=[
                pltpu.VMEM((SEQ, S_ROWS + X_ROWS, COLS), BF16),
                pltpu.VMEM((W_ROWS, PB), BF16),
                pltpu.SemaphoreType.DMA((5, PIECES)),
                pltpu.SemaphoreType.DMA,
            ],
        ),
        out_shape=[
            jax.ShapeDtypeStruct((SEQ, S_ROWS + X_ROWS, COLS), BF16),
            jax.ShapeDtypeStruct((W_ROWS, PB), BF16),
        ],
        compiler_params=params(),
        name="pack",
    )(core, tok, spec, tb["perm"], *weights, gain)


def conv_kernel(
    msg_hbm, skip_ref, row_fwd_ref, row_inv_ref, cos_ref, sin_ref, fwd_ref, inv_ref,
    out_ref, msg_ref, x_f, spec_f, conv_f, sem,
):
    def spec_copy(part):
        devs, rows = pl.ds(part * 4, 4), pl.ds(0, S_ROWS)
        return pltpu.make_async_copy(msg_hbm.at[devs, rows, :], msg_ref.at[devs, rows, :], sem.at[part])

    rows = pl.ds(S_ROWS, X_ROWS)
    x_copy = pltpu.make_async_copy(msg_hbm.at[:, rows, :], msg_ref.at[:, rows, :], sem.at[8])
    x_copy.start()
    for part in range(SEQ // 4):
        spec_copy(part).start()
    x_copy.wait()
    for q in range(4):
        x_q = msg_ref[:, S_ROWS:, q * 128 : q * 128 + 128]
        x_f[q] = x_q.reshape(AROWS // 2 * OWN, 128).astype(F32)

    @pl.loop(0, SEQ // 4)
    def _(part):
        rows = pl.ds(pl.multiple_of(part * 256, 256), 256)
        spec_copy(part).wait()
        for k in range(2):
            for r in range(4):
                lanes = slice(r * 128, r * 128 + 128)
                block = msg_ref[pl.ds(part * 4, 4), k * 64 : k * 64 + 64, lanes]
                spec_f[k, r, rows, :] = block.reshape(256, 128).astype(F32)

    @pl.loop(0, OWN, unroll=4)
    def _(h):
        every = pl.ds(h, AROWS // 2, stride=OWN)
        x_h = jnp.concatenate([x_f[q, every, :] for q in range(4)], 1).astype(BF16)
        f = dot(row_fwd_ref[...], x_h)
        blocks = [(n * 16, n * 16 + 16) for n in range(AROWS // 16)]
        sides = []
        for q in range(4):
            lanes = slice(q * 128, q * 128 + 128)
            parts = []
            for lo, hi in blocks:
                co, si = cos_ref[lo:hi, lanes], sin_ref[lo:hi, lanes]
                f0, f1 = f[lo:hi, lanes], f[AROWS + lo : AROWS + hi, lanes]
                y0, y1 = f0 * co + f1 * si, f1 * co - f0 * si
                parts.append(jnp.concatenate([y0, y1], 1).astype(BF16))
            sides.append(dot(jnp.concatenate(parts, 0), fwd_ref[q]))

        parts = [[] for _ in range(4)]
        for lo, hi in blocks:
            re = [sides[q][lo:hi, 0:128] for q in range(4)]
            im = [sides[q][lo:hi, 128:256] for q in range(4)]
            t0r, t0i = re[0] + re[2], im[0] + im[2]
            t1r, t1i = re[0] - re[2], im[0] - im[2]
            t2r, t2i = re[1] + re[3], im[1] + im[3]
            t3r, t3i = re[1] - re[3], im[1] - im[3]
            zr = [t0r + t2r, t1r + t3i, t0r - t2r, t1r - t3i]
            zi = [t0i + t2i, t1i - t3r, t0i - t2i, t1i + t3r]
            pr, pi = [], []
            srows = pl.ds(h + lo * OWN, 16, stride=OWN)
            for r in range(4):
                sr, si = spec_f[0, r, srows, :], spec_f[1, r, srows, :]
                pr.append(zr[r] * sr - zi[r] * si)
                pi.append(zr[r] * si + zi[r] * sr)
            u0r, u0i = pr[0] + pr[2], pi[0] + pi[2]
            u1r, u1i = pr[0] - pr[2], pi[0] - pi[2]
            u2r, u2i = pr[1] + pr[3], pi[1] + pi[3]
            u3r, u3i = pr[1] - pr[3], pi[1] - pi[3]
            qr = [u0r + u2r, u1r - u3i, u0r - u2r, u1r + u3i]
            qi = [u0i + u2i, u1i + u3r, u0i - u2i, u1i - u3r]
            for q in range(4):
                parts[q].append(jnp.concatenate([qr[q], qi[q]], 1).astype(BF16))

        columns = []
        for q in range(4):
            lanes = slice(q * 128, q * 128 + 128)
            back = dot(jnp.concatenate(parts[q], 0), inv_ref[q])
            v0, v1 = [], []
            for lo, hi in blocks:
                co, si = cos_ref[lo:hi, lanes], sin_ref[lo:hi, lanes]
                b0, b1 = back[lo:hi, 0:128], back[lo:hi, 128:256]
                v0.append((b0 * co - b1 * si).astype(BF16))
                v1.append((b1 * co + b0 * si).astype(BF16))
            columns.append(jnp.concatenate(v0 + v1, 0))
        conv = dot(row_inv_ref[...], jnp.concatenate(columns, 1)) * (1.0 / SPAN)
        for q in range(4):
            conv_f[q, every, :] = conv[:, q * 128 : q * 128 + 128]

    skip = skip_ref[...].reshape(1, OWN, 1)

    @pl.loop(0, 8)
    def _(part):
        a0 = pl.multiple_of(part * 16, 16)
        kept = []
        for q in range(4):
            conv = conv_f[q, pl.ds(a0 * OWN, 16 * OWN), :].astype(BF16).astype(F32)
            x_q = msg_ref[pl.ds(part * 4, 4), S_ROWS:, q * 128 : q * 128 + 128].astype(F32)
            kept.append(conv.reshape(16, OWN, 128) + skip * x_q.reshape(16, OWN, 128))
        for half in range(2):
            lanes = slice(half * 64, half * 64 + 64)
            pairs = [
                jnp.concatenate([kept[2 * n][:, :, lanes], kept[2 * n + 1][:, :, lanes]], 2)
                for n in range(2)
            ]
            out_ref[pl.ds(a0, 16), half] = jnp.concatenate(pairs, 1).astype(BF16)


def in_vmem(value):
    return pltpu.with_memory_space_constraint(value, pltpu.VMEM)


def convolve(msg, skip, tb):
    vmem = pl.BlockSpec(memory_space=pltpu.VMEM)
    return pl.pallas_call(
        conv_kernel,
        in_specs=[pl.BlockSpec(memory_space=pltpu.HBM)] + [vmem] * 7,
        out_specs=vmem,
        out_shape=jax.ShapeDtypeStruct((AROWS // 2, 2, 16, 128), BF16),
        scratch_shapes=[
            pltpu.VMEM((SEQ, S_ROWS + X_ROWS, COLS), BF16),
            pltpu.VMEM((4, AROWS // 2 * OWN, 128), F32),
            pltpu.VMEM((2, 4, AROWS * OWN, 128), F32),
            pltpu.VMEM((4, AROWS // 2 * OWN, 128), F32),
            pltpu.SemaphoreType.DMA((9,)),
        ],
        compiler_params=pltpu.CompilerParams(vmem_limit_bytes=30 * 1024 * 1024),
        name="convolve",
    )(msg, in_vmem(skip), *(in_vmem(jnp.asarray(tb[n])) for n in ("row_fwd", "row_inv", "cos", "sin", "fwd", "inv")))


def mlp_kernel(
    x_ref, w_hbm, unperm_ref, out_ref, w_ref, stream_s, gate_s, up_s, down_s, gain_s, sem,
):
    def second_copy(j):
        part = pl.ds(0, 1536)
        return pltpu.make_async_copy(w_hbm.at[j, :, part, :], w_ref.at[j, :, part, :], sem.at[j])

    part = pl.ds(1536, W_ROWS - 1536)
    first_copy = pltpu.make_async_copy(w_hbm.at[:, :, part, :], w_ref.at[:, :, part, :], sem.at[8])
    first_copy.start()
    for j in range(8):
        second_copy(j).start()

    total = jnp.zeros((1, TOK), F32)
    for i in range(8):
        rows = x_ref[:, i].astype(F32)
        rows = jnp.concatenate([rows[:, 0:8, :], rows[:, 8:16, :]], 2).reshape(WIDTH, TOK)
        stream_s[i] = rows
        total = total + jnp.sum(rows * rows, axis=0, keepdims=True)
    scale = lax.rsqrt(total * (1.0 / D) + 1e-05)
    first_copy.wait()
    parts = jnp.concatenate([w_ref[i, 0, 1920:1936, :] for i in range(8)], 1)
    gain_s[...] = lax.dot_general(
        parts, jnp.ones((16, 128), BF16), (((0,), (0,)), ((), ())), preferred_element_type=F32
    )

    @pl.loop(0, 8, unroll=8)
    def _(i):
        gain = gain_s[pl.ds(pl.multiple_of(i * WIDTH, WIDTH), WIDTH), :]
        normed = (stream_s[i] * scale * jnp.concatenate([gain, gain], 1)).astype(BF16)
        rows = pl.ds(pl.multiple_of(i * PIECE, PIECE), PIECE)
        for half in range(2):
            mid = dot(w_ref[i, half, 1536:1792, :], normed).astype(BF16)
            for n in range(4):
                gate_s[half * 4 + n, rows, :] = mid[n * PIECE : n * PIECE + PIECE]
                n1 = 128 + n * PIECE
                up_s[half * 4 + n, rows, :] = mid[n1 : n1 + PIECE]

    def block(j):
        gate_in, up_in = gate_s[j], up_s[j]
        acts, lefts = [], []
        for half in range(2):
            for n in range(2):
                r0 = n * 256
                gate = dot(w_ref[j, half, r0 : r0 + 256, :], gate_in)
                upper = dot(w_ref[j, half, 512 + r0 : 768 + r0, :], up_in)
                acts.append((jax.nn.gelu(gate, approximate=True) * upper).astype(BF16))
                lefts.append(w_ref[j, half, 1024 + r0 : 1280 + r0, :])
        mid = dot(jnp.concatenate(lefts, 1), jnp.concatenate(acts, 0)).astype(BF16)
        rows = pl.ds(pl.multiple_of(j * PIECE, PIECE), PIECE)
        for o in range(8):
            down_s[o, rows, :] = mid[o * PIECE : o * PIECE + PIECE]

    @pl.loop(0, 2)
    def _(group):
        for n in range(4):
            second_copy(group * 4 + n).wait()
        for n in range(4):
            block(group * 4 + n)

    unperm = unperm_ref[...]

    @pl.loop(0, 8, unroll=8)
    def _(o):
        down = down_s[o]
        res = jnp.concatenate([dot(w_ref[o, half, 1792:1920, :], down) for half in range(2)], 0)
        res = (stream_s[o] + res).astype(BF16)
        out_ref[o] = dot_nt(unperm, res).astype(BF16)


def in_vmem(value):
    return pltpu.with_memory_space_constraint(value, pltpu.VMEM)


def mlp(x, weights, tb):
    vmem = pl.BlockSpec(memory_space=pltpu.VMEM)
    return pl.pallas_call(
        mlp_kernel,
        in_specs=[vmem, pl.BlockSpec(memory_space=pltpu.HBM), vmem],
        out_specs=vmem,
        out_shape=jax.ShapeDtypeStruct((8, TOK, WIDTH), BF16),
        scratch_shapes=[
            pltpu.VMEM((8, 2, W_ROWS, PB), BF16),
            pltpu.VMEM((8, WIDTH, TOK), F32),
            pltpu.VMEM((8, PB, TOK), BF16),
            pltpu.VMEM((8, PB, TOK), BF16),
            pltpu.VMEM((8, PB, TOK), BF16),
            pltpu.VMEM((D, 128), F32),
            pltpu.SemaphoreType.DMA((9,)),
        ],
        compiler_params=pltpu.CompilerParams(vmem_limit_bytes=40 * 1024 * 1024),
        name="mlp",
    )(in_vmem(x), weights, in_vmem(jnp.asarray(tb["unperm"])))


def exchange(value, axis):
    return lax.all_to_all(value, axis, split_axis=0, concat_axis=0, tiled=True)


SEQ_AXES = ("chip", "core")


def per_device(
    tokens, spectrum, skip_gain, norm_gain,
    gate_first, up_first, gate_second, up_second, down_first, down_second,
):
    tb = tables()
    core = lax.axis_index("core").astype(jnp.int32).reshape(1)
    raw = (gate_first, up_first, gate_second, up_second, down_first, down_second)
    msg, weights = pack(tokens, spectrum, core, raw, norm_gain.reshape(1, WIDTH), tb)
    weights = lax.all_gather(weights, ("chan", "core"), axis=0, tiled=False)
    weights = weights.reshape(8, 2, W_ROWS, PB)
    skip = lax.dynamic_slice(skip_gain, (lax.axis_index(SEQ_AXES) * OWN,), (OWN,)).reshape(OWN, 1)
    stream = convolve(exchange(msg, SEQ_AXES), skip, tb).reshape(SEQ * CHAN, 16, 128)
    stream = exchange(stream, SEQ_AXES + ("chan",)).reshape(SEQ, CHAN, 16, 128)
    out = mlp(stream, weights, tb)
    return exchange(out, "chan").reshape(ROWS_DEV * COLS, WIDTH)


def solution(mesh):
    split = jax.sharding.Mesh(mesh.devices.reshape(SEQ // 2, 2, CHAN), ("chip", "core", "chan"))
    in_specs = (
        P(SEQ_AXES, "chan"),
        P(None, SEQ_AXES, None, "chan"),
        P("chan"),
        P("chan"),
        P("chan", None, None),
        P("chan", None, None),
        P("chan", None, None),
        P("chan", None, None),
        P("chan", None, None),
        P("chan", None, None),
    )
    return jax.shard_map(
        per_device, mesh=split, in_specs=in_specs, out_specs=P(SEQ_AXES, "chan"), check_vma=False
    )
```

```python
import functools

import jax
import jax.numpy as jnp
import ml_dtypes
import numpy as np
from jax import lax
from jax.experimental import pallas as pl
from jax.experimental.pallas import tpu as pltpu
from jax.sharding import PartitionSpec as P

D = 2048
COLS = 512
AROWS = 256
SPAN = 131072
SEQ = 32
CHAN = 8
OWN = 8
WIDTH = 256
PB = 256
HB = 1024
PIECE = 32
ROWS_DEV = 4
TOK = 256
S_ROWS = 128
X_ROWS = 32
F32 = jnp.float32
BF16 = jnp.bfloat16
VMEM_LIMIT = 56 * 1024 * 1024


def bf16(values):
    return np.asarray(values, np.float64).astype(np.float32).astype(ml_dtypes.bfloat16)


def angle(product, period):
    return 2.0 * np.pi / period * (product % period)


@functools.lru_cache(None)
def tables():
    cols = np.arange(COLS)
    perm_cols = (cols % 128) * 4 + cols // 128
    perm = np.zeros((COLS, COLS))
    perm[cols, perm_cols] = 1.0
    place = np.arange(TOK)
    token = 4 * (place % 64) + 2 * (place // 128) + place // 64 % 2
    unperm = np.zeros((TOK, TOK))
    unperm[token, place] = 1.0
    c = np.arange(AROWS)
    rows = angle(c[:, None] * np.arange(AROWS // 2)[None, :], AROWS)
    row_fwd = np.concatenate([np.cos(rows), -np.sin(rows)], 0)
    row_inv = row_fwd.T
    theta = angle(c[:, None] * perm_cols[None, :], SPAN)
    fwd, inv = [], []
    for q in range(4):
        ang = angle((4 * np.arange(128) + q)[:, None] * np.arange(128)[None, :], COLS)
        co, si = np.cos(ang), np.sin(ang)
        fwd.append(np.block([[co, -si], [si, co]]))
        inv.append(np.block([[co.T, si.T], [-si.T, co.T]]))
    return dict(
        perm=bf16(perm),
        unperm=bf16(unperm),
        row_fwd=bf16(row_fwd),
        row_inv=bf16(row_inv),
        cos=np.cos(theta).astype(np.float32),
        sin=np.sin(theta).astype(np.float32),
        fwd=bf16(np.stack(fwd)),
        inv=bf16(np.stack(inv)),
    )


def dot(a, b):
    return jnp.dot(a, b, preferred_element_type=F32)


def dot_nt(a, b):
    return lax.dot_general(a, b, (((1,), (1,)), ((), ())), preferred_element_type=F32)


def params():
    return pltpu.CompilerParams(vmem_limit_bytes=VMEM_LIMIT)


W_ROWS = 1936
PIECES = 4


def turn_weights(g1_ref, u1_ref, g2_ref, u2_ref, d1_ref, d2_ref, gain_ref, out_ref):
    tiles = [g2_ref[0, :, 0:256], g2_ref[0, :, 256:512], u2_ref[0, :, 0:256], u2_ref[0, :, 256:512]]
    tiles += [d1_ref[0, 0:256, :], d1_ref[0, 256:512, :]]
    for n, tile in enumerate(tiles):
        out_ref[n * 256 : n * 256 + 256, :] = tile.T
    for n, ref in enumerate((g1_ref, u1_ref, d2_ref)):
        r0 = 1536 + n * 128
        out_ref[r0 : r0 + 128, :] = ref[0].T
    gain = gain_ref[...]
    high = gain.astype(BF16).astype(F32)
    mid = (gain - high).astype(BF16).astype(F32)
    low = gain - high - mid
    out_ref[1920:, :] = jnp.concatenate([high, mid, low, jnp.zeros((13, PB), F32)], 0).astype(BF16)


def pack_kernel(core_ref, tok_ref, spec_ref, perm_ref, *refs):
    weight_refs, (msg_ref, w_ref, msg_s, w_s, msg_sem, w_sem) = refs[:7], refs[7:]
    step = pl.program_id(0)

    def turned(tiles):
        tiles = [tile.T.astype(F32).reshape(SEQ, OWN, COLS) for tile in tiles]
        return jnp.concatenate(tiles, 1).astype(BF16)

    def copies(at):
        rows = pl.ds(pl.multiple_of(at * 32, 32), 32)
        for n in range(PIECES):
            part = pl.ds(n * (SEQ // PIECES), SEQ // PIECES)
            yield pltpu.make_async_copy(
                msg_s.at[part, rows, :], msg_ref.at[part, rows, :], msg_sem.at[at, n]
            )

    w_copy = pltpu.make_async_copy(w_s, w_ref, w_sem)

    @pl.when(step < 4)
    def _():
        for n in range(2):
            rows = pl.ds(pl.multiple_of(step * 32 + n * 16, 16), 16)
            msg_s[:, rows, :] = turned([spec_ref[2 * n], spec_ref[2 * n + 1]])

    @pl.when(step == 4)
    def _():
        perm = perm_ref[...]
        for n in range(2):
            tiles = [dot(perm, tok_ref[2 * n + m]).astype(BF16) for m in range(2)]
            msg_s[:, S_ROWS + n * 16 : S_ROWS + n * 16 + 16, :] = turned(tiles)

    for copy in copies(step):
        copy.start()

    @pl.when(step == 1)
    def _():
        turn_weights(*weight_refs, w_s)
        w_copy.start()

    @pl.when(step == 4)
    def _():
        for at in range(5):
            for copy in copies(at):
                copy.wait()
        w_copy.wait()


def pack(tokens, spectrum, core, weights, gain, tb):
    tok = tokens.reshape(ROWS_DEV, COLS, WIDTH)
    spec = spectrum.reshape(16, COLS, WIDTH)
    whole = lambda *shape: pl.BlockSpec(shape, lambda g, core: (0,) * len(shape))
    cols = lambda n: pl.BlockSpec((1, PB, n), lambda g, core: (0, 0, core[0]))
    hbm = pl.BlockSpec(memory_space=pltpu.HBM)
    return pl.pallas_call(
        pack_kernel,
        grid_spec=pltpu.PrefetchScalarGridSpec(
            num_scalar_prefetch=1,
            grid=(5,),
            in_specs=[
                whole(ROWS_DEV, COLS, WIDTH),
                pl.BlockSpec((4, COLS, WIDTH), lambda g, core: (jnp.minimum(g, 3), 0, 0)),
                whole(COLS, COLS),
                cols(128),
                cols(128),
                cols(512),
                cols(512),
                pl.BlockSpec((1, 512, PB), lambda g, core: (0, core[0], 0)),
                cols(128),
                whole(1, WIDTH),
            ],
            out_specs=[hbm, hbm],
            scratch_shapes=[
                pltpu.VMEM((SEQ, S_ROWS + X_ROWS, COLS), BF16),
                pltpu.VMEM((W_ROWS, PB), BF16),
                pltpu.SemaphoreType.DMA((5, PIECES)),
                pltpu.SemaphoreType.DMA,
            ],
        ),
        out_shape=[
            jax.ShapeDtypeStruct((SEQ, S_ROWS + X_ROWS, COLS), BF16),
            jax.ShapeDtypeStruct((W_ROWS, PB), BF16),
        ],
        compiler_params=params(),
        name="pack",
    )(core, tok, spec, tb["perm"], *weights, gain)


def conv_kernel(
    msg_hbm, skip_ref, row_fwd_ref, row_inv_ref, cos_ref, sin_ref, fwd_ref, inv_ref,
    out_ref, msg_ref, x_f, spec_f, conv_f, sem,
):
    def spec_copy(part):
        devs, rows = pl.ds(part * 4, 4), pl.ds(0, S_ROWS)
        return pltpu.make_async_copy(msg_hbm.at[devs, rows, :], msg_ref.at[devs, rows, :], sem.at[part])

    rows = pl.ds(S_ROWS, X_ROWS)
    x_copy = pltpu.make_async_copy(msg_hbm.at[:, rows, :], msg_ref.at[:, rows, :], sem.at[8])
    x_copy.start()
    for part in range(SEQ // 4):
        spec_copy(part).start()
    x_copy.wait()
    for q in range(4):
        x_q = msg_ref[:, S_ROWS:, q * 128 : q * 128 + 128]
        x_f[q] = x_q.reshape(AROWS // 2 * OWN, 128).astype(F32)

    @pl.loop(0, SEQ // 4)
    def _(part):
        rows = pl.ds(pl.multiple_of(part * 256, 256), 256)
        spec_copy(part).wait()
        for k in range(2):
            for r in range(4):
                lanes = slice(r * 128, r * 128 + 128)
                block = msg_ref[pl.ds(part * 4, 4), k * 64 : k * 64 + 64, lanes]
                spec_f[k, r, rows, :] = block.reshape(256, 128).astype(F32)

    @pl.loop(0, OWN, unroll=4)
    def _(h):
        every = pl.ds(h, AROWS // 2, stride=OWN)
        x_h = jnp.concatenate([x_f[q, every, :] for q in range(4)], 1).astype(BF16)
        f = dot(row_fwd_ref[...], x_h)
        blocks = [(n * 16, n * 16 + 16) for n in range(AROWS // 16)]
        sides = []
        for q in range(4):
            lanes = slice(q * 128, q * 128 + 128)
            parts = []
            for lo, hi in blocks:
                co, si = cos_ref[lo:hi, lanes], sin_ref[lo:hi, lanes]
                f0, f1 = f[lo:hi, lanes], f[AROWS + lo : AROWS + hi, lanes]
                y0, y1 = f0 * co + f1 * si, f1 * co - f0 * si
                parts.append(jnp.concatenate([y0, y1], 1).astype(BF16))
            sides.append(dot(jnp.concatenate(parts, 0), fwd_ref[q]))

        parts = [[] for _ in range(4)]
        for lo, hi in blocks:
            re = [sides[q][lo:hi, 0:128] for q in range(4)]
            im = [sides[q][lo:hi, 128:256] for q in range(4)]
            t0r, t0i = re[0] + re[2], im[0] + im[2]
            t1r, t1i = re[0] - re[2], im[0] - im[2]
            t2r, t2i = re[1] + re[3], im[1] + im[3]
            t3r, t3i = re[1] - re[3], im[1] - im[3]
            zr = [t0r + t2r, t1r + t3i, t0r - t2r, t1r - t3i]
            zi = [t0i + t2i, t1i - t3r, t0i - t2i, t1i + t3r]
            pr, pi = [], []
            srows = pl.ds(h + lo * OWN, 16, stride=OWN)
            for r in range(4):
                sr, si = spec_f[0, r, srows, :], spec_f[1, r, srows, :]
                pr.append(zr[r] * sr - zi[r] * si)
                pi.append(zr[r] * si + zi[r] * sr)
            u0r, u0i = pr[0] + pr[2], pi[0] + pi[2]
            u1r, u1i = pr[0] - pr[2], pi[0] - pi[2]
            u2r, u2i = pr[1] + pr[3], pi[1] + pi[3]
            u3r, u3i = pr[1] - pr[3], pi[1] - pi[3]
            qr = [u0r + u2r, u1r - u3i, u0r - u2r, u1r + u3i]
            qi = [u0i + u2i, u1i + u3r, u0i - u2i, u1i - u3r]
            for q in range(4):
                parts[q].append(jnp.concatenate([qr[q], qi[q]], 1).astype(BF16))

        columns = []
        for q in range(4):
            lanes = slice(q * 128, q * 128 + 128)
            back = dot(jnp.concatenate(parts[q], 0), inv_ref[q])
            v0, v1 = [], []
            for lo, hi in blocks:
                co, si = cos_ref[lo:hi, lanes], sin_ref[lo:hi, lanes]
                b0, b1 = back[lo:hi, 0:128], back[lo:hi, 128:256]
                v0.append((b0 * co - b1 * si).astype(BF16))
                v1.append((b1 * co + b0 * si).astype(BF16))
            columns.append(jnp.concatenate(v0 + v1, 0))
        conv = dot(row_inv_ref[...], jnp.concatenate(columns, 1)) * (1.0 / SPAN)
        for q in range(4):
            conv_f[q, every, :] = conv[:, q * 128 : q * 128 + 128]

    skip = skip_ref[...].reshape(1, OWN, 1)

    @pl.loop(0, 8)
    def _(part):
        a0 = pl.multiple_of(part * 16, 16)
        kept = []
        for q in range(4):
            conv = conv_f[q, pl.ds(a0 * OWN, 16 * OWN), :].astype(BF16).astype(F32)
            x_q = msg_ref[pl.ds(part * 4, 4), S_ROWS:, q * 128 : q * 128 + 128].astype(F32)
            kept.append(conv.reshape(16, OWN, 128) + skip * x_q.reshape(16, OWN, 128))
        for half in range(2):
            lanes = slice(half * 64, half * 64 + 64)
            pairs = [
                jnp.concatenate([kept[2 * n][:, :, lanes], kept[2 * n + 1][:, :, lanes]], 2)
                for n in range(2)
            ]
            out_ref[pl.ds(a0, 16), half] = jnp.concatenate(pairs, 1).astype(BF16)


def in_vmem(value):
    return pltpu.with_memory_space_constraint(value, pltpu.VMEM)


def convolve(msg, skip, tb):
    vmem = pl.BlockSpec(memory_space=pltpu.VMEM)
    return pl.pallas_call(
        conv_kernel,
        in_specs=[pl.BlockSpec(memory_space=pltpu.HBM)] + [vmem] * 7,
        out_specs=vmem,
        out_shape=jax.ShapeDtypeStruct((AROWS // 2, 2, 16, 128), BF16),
        scratch_shapes=[
            pltpu.VMEM((SEQ, S_ROWS + X_ROWS, COLS), BF16),
            pltpu.VMEM((4, AROWS // 2 * OWN, 128), F32),
            pltpu.VMEM((2, 4, AROWS * OWN, 128), F32),
            pltpu.VMEM((4, AROWS // 2 * OWN, 128), F32),
            pltpu.SemaphoreType.DMA((9,)),
        ],
        compiler_params=pltpu.CompilerParams(vmem_limit_bytes=30 * 1024 * 1024),
        name="convolve",
    )(msg, in_vmem(skip), *(in_vmem(jnp.asarray(tb[n])) for n in ("row_fwd", "row_inv", "cos", "sin", "fwd", "inv")))


def mlp_kernel(place_ref, x_ref, unperm_ref, *refs):
    held = refs[0:4], refs[4:8]
    out_ref, w_ref, stream_s, gate_s, up_s, down_s, gain_s, sem = refs[8:]
    y, x, core = place_ref[0], place_ref[1], place_ref[2]

    def block_of(n):
        return lax.rem(y + lax.rem(n, 2), 2) * 4 + lax.rem(x - n // 2 + 4, 4)

    def copies(part, k):
        rows = (pl.ds(1536, W_ROWS - 1536), pl.ds(0, 1536))[part]
        for twin in range(2):
            half = lax.rem(core + twin, 2)
            yield pltpu.make_async_copy(
                held[twin][k].at[:, rows, :],
                w_ref.at[pl.ds(2 * k, 2), half, rows, :],
                sem.at[part, k, twin],
            )

    for part in range(2):
        for k in range(4):
            for copy in copies(part, k):
                copy.start()

    total = jnp.zeros((1, TOK), F32)
    for i in range(8):
        rows = x_ref[:, i].astype(F32)
        rows = jnp.concatenate([rows[:, 0:8, :], rows[:, 8:16, :]], 2).reshape(WIDTH, TOK)
        stream_s[i] = rows
        total = total + jnp.sum(rows * rows, axis=0, keepdims=True)
    scale = lax.rsqrt(total * (1.0 / D) + 1e-05)
    for k in range(4):
        for copy in copies(0, k):
            copy.wait()
    parts = jnp.concatenate([w_ref[n, 0, 1920:1936, :] for n in range(8)], 1)
    gain_s[...] = lax.dot_general(
        parts, jnp.ones((16, 128), BF16), (((0,), (0,)), ((), ())), preferred_element_type=F32
    )

    for n in range(8):
        i = block_of(n)
        gain = gain_s[n * WIDTH : n * WIDTH + WIDTH, :]
        normed = (stream_s[i] * scale * jnp.concatenate([gain, gain], 1)).astype(BF16)
        rows = pl.ds(pl.multiple_of(i * PIECE, PIECE), PIECE)
        for half in range(2):
            mid = dot(w_ref[n, half, 1536:1792, :], normed).astype(BF16)
            for m in range(4):
                gate_s[half * 4 + m, rows, :] = mid[m * PIECE : m * PIECE + PIECE]
                m1 = 128 + m * PIECE
                up_s[half * 4 + m, rows, :] = mid[m1 : m1 + PIECE]

    def block(n):
        j = block_of(n)
        gate_in, up_in = gate_s[j], up_s[j]
        acts, lefts = [], []
        for half in range(2):
            for m in range(2):
                r0 = m * 256
                gate = dot(w_ref[n, half, r0 : r0 + 256, :], gate_in)
                upper = dot(w_ref[n, half, 512 + r0 : 768 + r0, :], up_in)
                acts.append((jax.nn.gelu(gate, approximate=True) * upper).astype(BF16))
                lefts.append(w_ref[n, half, 1024 + r0 : 1280 + r0, :])
        mid = dot(jnp.concatenate(lefts, 1), jnp.concatenate(acts, 0)).astype(BF16)
        rows = pl.ds(pl.multiple_of(j * PIECE, PIECE), PIECE)
        for o in range(8):
            down_s[o, rows, :] = mid[o * PIECE : o * PIECE + PIECE]

    for group in range(2):
        for k in range(2):
            for copy in copies(1, group * 2 + k):
                copy.wait()
        for n in range(4):
            block(group * 4 + n)

    unperm = unperm_ref[...]
    for n in range(8):
        o = block_of(n)
        down = down_s[o]
        res = jnp.concatenate([dot(w_ref[n, half, 1792:1920, :], down) for half in range(2)], 0)
        res = (stream_s[o] + res).astype(BF16)
        out_ref[o] = dot_nt(unperm, res).astype(BF16)


def mlp(place, x, held, twins, tb):
    vmem = pl.BlockSpec(memory_space=pltpu.VMEM)
    hbm = pl.BlockSpec(memory_space=pltpu.HBM)
    return pl.pallas_call(
        mlp_kernel,
        in_specs=[pl.BlockSpec(memory_space=pltpu.SMEM), vmem, vmem] + [hbm] * 8,
        out_specs=vmem,
        out_shape=jax.ShapeDtypeStruct((8, TOK, WIDTH), BF16),
        scratch_shapes=[
            pltpu.VMEM((8, 2, W_ROWS, PB), BF16),
            pltpu.VMEM((8, WIDTH, TOK), F32),
            pltpu.VMEM((8, PB, TOK), BF16),
            pltpu.VMEM((8, PB, TOK), BF16),
            pltpu.VMEM((8, PB, TOK), BF16),
            pltpu.VMEM((D, 128), F32),
            pltpu.SemaphoreType.DMA((2, 4, 2)),
        ],
        compiler_params=pltpu.CompilerParams(vmem_limit_bytes=40 * 1024 * 1024),
        name="mlp",
    )(place, in_vmem(x), in_vmem(jnp.asarray(tb["unperm"])), *held, *twins)


def exchange(value, axis):
    return lax.all_to_all(value, axis, split_axis=0, concat_axis=0, tiled=True)


SEQ_AXES = ("chip", "core")


def per_device(
    tokens, spectrum, skip_gain, norm_gain,
    gate_first, up_first, gate_second, up_second, down_first, down_second,
):
    tb = tables()
    core = lax.axis_index("core").astype(jnp.int32).reshape(1)
    raw = (gate_first, up_first, gate_second, up_second, down_first, down_second)
    msg, weights = pack(tokens, spectrum, core, raw, norm_gain.reshape(1, WIDTH), tb)
    other = lax.ppermute(weights, "chan", [(n, n ^ 4) for n in range(CHAN)])
    pair = jnp.stack([weights, other])
    held = [pair]
    for k in range(1, 4):
        held.append(lax.ppermute(pair, "chan", [(n, n // 4 * 4 + (n + k) % 4) for n in range(CHAN)]))
    twins = [lax.ppermute(part, "core", [(0, 1), (1, 0)]) for part in held]
    skip = lax.dynamic_slice(skip_gain, (lax.axis_index(SEQ_AXES) * OWN,), (OWN,)).reshape(OWN, 1)
    stream = convolve(exchange(msg, SEQ_AXES), skip, tb).reshape(SEQ * CHAN, 16, 128)
    stream = exchange(stream, SEQ_AXES + ("chan",)).reshape(SEQ, CHAN, 16, 128)
    chan = lax.axis_index("chan")
    place = jnp.stack([chan // 4, chan % 4, lax.axis_index("core")]).astype(jnp.int32)
    out = mlp(place, stream, held, twins, tb)
    return exchange(out, "chan").reshape(ROWS_DEV * COLS, WIDTH)


def solution(mesh):
    split = jax.sharding.Mesh(mesh.devices.reshape(SEQ // 2, 2, CHAN), ("chip", "core", "chan"))
    in_specs = (
        P(SEQ_AXES, "chan"),
        P(None, SEQ_AXES, None, "chan"),
        P("chan"),
        P("chan"),
        P("chan", None, None),
        P("chan", None, None),
        P("chan", None, None),
        P("chan", None, None),
        P("chan", None, None),
        P("chan", None, None),
    )
    return jax.shard_map(
        per_device, mesh=split, in_specs=in_specs, out_specs=P(SEQ_AXES, "chan"), check_vma=False
    )
```

```python
import functools

import jax
import jax.numpy as jnp
import ml_dtypes
import numpy as np
from jax import lax
from jax.experimental import pallas as pl
from jax.experimental.pallas import tpu as pltpu
from jax.sharding import PartitionSpec as P

D = 2048
COLS = 512
AROWS = 256
SPAN = 131072
SEQ = 32
CHAN = 8
OWN = 8
WIDTH = 256
PB = 256
HB = 1024
PIECE = 32
ROWS_DEV = 4
TOK = 256
S_ROWS = 128
X_ROWS = 32
F32 = jnp.float32
BF16 = jnp.bfloat16
VMEM_LIMIT = 56 * 1024 * 1024


def bf16(values):
    return np.asarray(values, np.float64).astype(np.float32).astype(ml_dtypes.bfloat16)


def angle(product, period):
    return 2.0 * np.pi / period * (product % period)


@functools.lru_cache(None)
def tables():
    cols = np.arange(COLS)
    perm_cols = (cols % 128) * 4 + cols // 128
    perm = np.zeros((COLS, COLS))
    perm[cols, perm_cols] = 1.0
    place = np.arange(TOK)
    token = 4 * (place % 64) + 2 * (place // 128) + place // 64 % 2
    unperm = np.zeros((TOK, TOK))
    unperm[token, place] = 1.0
    half = AROWS // 2
    c = np.arange(half + 16)
    rows = angle(c[:, None] * np.arange(half)[None, :], AROWS)
    cos_a, sin_a = np.cos(rows) * (c <= half)[:, None], -np.sin(rows) * (c <= half)[:, None]
    row_fwd = np.concatenate([cos_a, sin_a], 0)
    row_inv = np.concatenate([cos_a[:half], cos_a[half : half + 1], sin_a[1:half]], 0).T
    theta = angle(c[:, None] * perm_cols[None, :], SPAN)
    fwd, inv = [], []
    for q in range(4):
        ang = angle((4 * np.arange(128) + q)[:, None] * np.arange(128)[None, :], COLS)
        co, si = np.cos(ang), np.sin(ang)
        fwd.append(np.block([[co, -si], [si, co]]))
        inv.append(np.block([[co.T, si.T], [-si.T, co.T]]))
    return dict(
        perm=bf16(perm),
        unperm=bf16(unperm),
        row_fwd=bf16(row_fwd),
        row_inv=bf16(row_inv),
        cos=np.cos(theta).astype(np.float32),
        sin=np.sin(theta).astype(np.float32),
        flip=bf16(np.eye(256)[::-1]),
        fwd=bf16(np.stack(fwd)),
        inv=bf16(np.stack(inv)),
    )


def dot(a, b):
    return jnp.dot(a, b, preferred_element_type=F32)


def dot_nt(a, b):
    return lax.dot_general(a, b, (((1,), (1,)), ((), ())), preferred_element_type=F32)


def params():
    return pltpu.CompilerParams(vmem_limit_bytes=VMEM_LIMIT)


W_ROWS = 1936
PIECES = 4


def pack_kernel(core_ref, tok_hbm, spec_hbm, perm_hbm, *refs):
    weights_hbm, (msg_ref, w_ref), refs = refs[:7], refs[7:9], refs[9:]
    tok_s, spec_s, perm_s, g1_s, u1_s, g2_s, u2_s, d1_s, d2_s, gain_s, msg_s, w_s = refs[:12]
    in_sem, w_sem, out_sem = refs[12:]
    core = core_ref[0]

    def columns(n):
        return pl.ds(pl.multiple_of(core * n, n), n)

    def fetch(source, target, sem):
        return pltpu.make_async_copy(source, target, sem)

    def spec_fetch(n):
        return fetch(spec_hbm.at[pl.ds(4 * n, 4)], spec_s.at[pl.ds(4 * n, 4)], in_sem.at[n])

    raw = [
        fetch(ref.at[0, :, columns(target.shape[1])], target, w_sem.at[n])
        for n, (ref, target) in enumerate(zip(weights_hbm[:4], (g1_s, u1_s, g2_s, u2_s)))
    ]
    raw.append(fetch(weights_hbm[4].at[0, columns(512), :], d1_s, w_sem.at[4]))
    raw.append(fetch(weights_hbm[5].at[0, :, columns(128)], d2_s, w_sem.at[5]))
    raw.append(fetch(weights_hbm[6], gain_s, w_sem.at[6]))
    tokens = [fetch(tok_hbm, tok_s, in_sem.at[4]), fetch(perm_hbm, perm_s, in_sem.at[5])]
    for n in range(4):
        spec_fetch(n).start()
    for copy in raw + tokens:
        copy.start()

    def turned(tiles):
        tiles = [tile.T.astype(F32).reshape(SEQ, OWN, COLS) for tile in tiles]
        return jnp.concatenate(tiles, 1).astype(BF16)

    sent = []

    def send(rows, at):
        for n in range(PIECES):
            part = pl.ds(n * (SEQ // PIECES), SEQ // PIECES)
            copy = pltpu.make_async_copy(
                msg_s.at[part, rows, :], msg_ref.at[part, rows, :], out_sem.at[at, n]
            )
            copy.start()
            sent.append(copy)

    for n in range(4):
        spec_fetch(n).wait()
        for m in range(2):
            pair = turned([spec_s[4 * n + 2 * m], spec_s[4 * n + 2 * m + 1]])
            msg_s[:, n * 32 + m * 16 : n * 32 + m * 16 + 16, :] = pair
        send(pl.ds(n * 32, 32), n)

    for copy in raw:
        copy.wait()
    tiles = [g2_s[:, 0:256], g2_s[:, 256:512], u2_s[:, 0:256], u2_s[:, 256:512]]
    tiles += [d1_s[0:256, :], d1_s[256:512, :]]
    for n, tile in enumerate(tiles):
        w_s[n * 256 : n * 256 + 256, :] = tile.T
    for n, ref in enumerate((g1_s, u1_s, d2_s)):
        r0 = 1536 + n * 128
        w_s[r0 : r0 + 128, :] = ref[...].T
    gain = gain_s[...]
    high = gain.astype(BF16).astype(F32)
    mid = (gain - high).astype(BF16).astype(F32)
    low = gain - high - mid
    w_s[1920:, :] = jnp.concatenate([high, mid, low, jnp.zeros((13, PB), F32)], 0).astype(BF16)
    w_copy = pltpu.make_async_copy(w_s, w_ref, w_sem.at[7])
    w_copy.start()
    sent.append(w_copy)

    for copy in tokens:
        copy.wait()
    perm = perm_s[...]
    for m in range(2):
        pair = [dot(perm, tok_s[2 * m + n]).astype(BF16) for n in range(2)]
        msg_s[:, S_ROWS + m * 16 : S_ROWS + m * 16 + 16, :] = turned(pair)
    send(pl.ds(S_ROWS, X_ROWS), 4)
    for copy in sent:
        copy.wait()


def pack(tokens, spectrum, core, weights, gain, tb):
    tok = tokens.reshape(ROWS_DEV, COLS, WIDTH)
    spec = spectrum.reshape(16, COLS, WIDTH)
    hbm = pl.BlockSpec(memory_space=pltpu.HBM)
    shapes = [tok.shape, spec.shape, (COLS, COLS), (PB, 128), (PB, 128), (PB, 512), (PB, 512)]
    shapes += [(512, PB), (PB, 128)]
    return pl.pallas_call(
        pack_kernel,
        in_specs=[pl.BlockSpec(memory_space=pltpu.SMEM)] + [hbm] * 10,
        out_specs=[hbm, hbm],
        out_shape=[
            jax.ShapeDtypeStruct((SEQ, S_ROWS + X_ROWS, COLS), BF16),
            jax.ShapeDtypeStruct((W_ROWS, PB), BF16),
        ],
        scratch_shapes=[
            *(pltpu.VMEM(shape, BF16) for shape in shapes),
            pltpu.VMEM((1, WIDTH), F32),
            pltpu.VMEM((SEQ, S_ROWS + X_ROWS, COLS), BF16),
            pltpu.VMEM((W_ROWS, PB), BF16),
            pltpu.SemaphoreType.DMA((6,)),
            pltpu.SemaphoreType.DMA((8,)),
            pltpu.SemaphoreType.DMA((5, PIECES)),
        ],
        compiler_params=params(),
        name="pack",
    )(core, tok, spec, jnp.asarray(tb["perm"]), *weights, gain)


HALF = AROWS // 2
C_ROWS = HALF + 16
MIRROR = SEQ // 2
TABLES = ("row_fwd", "row_inv", "cos", "sin", "fwd", "inv", "flip")


def conv_kernel(msg_hbm, skip_ref, *refs):
    tables_hbm, out_ref, msg_ref = refs[:7], refs[7], refs[8]
    table_refs, (x_f, flip_f, spec_f, conv_f, sem, table_sem) = refs[9:16], refs[16:]
    row_fwd_ref, row_inv_ref, cos_ref, sin_ref, fwd_ref, inv_ref, flip_ref = table_refs

    def spec_copy(part):
        devs, rows = pl.ds(part * 4, 4), pl.ds(0, S_ROWS)
        return pltpu.make_async_copy(msg_hbm.at[devs, rows, :], msg_ref.at[devs, rows, :], sem.at[part])

    def table_copy(n):
        return pltpu.make_async_copy(tables_hbm[n], table_refs[n], table_sem.at[n])

    rows = pl.ds(S_ROWS, X_ROWS)
    x_copy = pltpu.make_async_copy(msg_hbm.at[:, rows, :], msg_ref.at[:, rows, :], sem.at[8])
    table_copy(6).start()
    for part in range(4, 8):
        spec_copy(part).start()
    for part in range(4):
        spec_copy(part).start()
    x_copy.start()
    for n in range(6):
        table_copy(n).start()

    flip_f[:, :, HALF * OWN :, :] = jnp.zeros((2, 4, OWN, 128), F32)
    spec_f[:, :, HALF * OWN :, :] = jnp.zeros((2, 4, 16 * OWN, 128), F32)
    table_copy(6).wait()
    flip = flip_ref[...]
    for part in range(4):
        spec_copy(part + 4).wait()
        for k in range(2):
            for pair in range(2):
                lanes = slice(pair * 256, pair * 256 + 256)
                block = msg_ref[MIRROR + part * 4 : MIRROR + part * 4 + 4, k * 64 : k * 64 + 64, lanes]
                turned = dot(block.reshape(256, 256), flip)
                rows = slice(part * 256, part * 256 + 256)
                flip_f[k, 2 - 2 * pair, rows, :] = turned[:, 0:128]
                flip_f[k, 3 - 2 * pair, rows, :] = turned[:, 128:256]

    for part in range(4):
        spec_copy(part).wait()

    @pl.loop(0, MIRROR, unroll=4)
    def _(dev):
        for k in range(2):
            for r in range(4):
                own = msg_ref[dev, k * 64 : k * 64 + 64, r * 128 : r * 128 + 128].astype(F32)
                mirror = [
                    flip_f[k, r, pl.ds(pl.multiple_of((HALF - j) * OWN - dev * 64, OWN), OWN), :]
                    for j in range(8)
                ]
                mirror = jnp.concatenate(mirror, 0)
                rows = pl.ds(pl.multiple_of(dev * 64, 64), 64)
                spec_f[k, r, rows, :] = own + mirror if k == 0 else own - mirror

    for k in range(2):
        for r in range(4):
            first = msg_ref[MIRROR, k * 64 : k * 64 + 16, r * 128 : r * 128 + 128].astype(F32)
            spec_f[k, r, HALF * OWN : HALF * OWN + OWN, :] = first[0:OWN]

    x_copy.wait()
    for q in range(4):
        x_q = msg_ref[:, S_ROWS:, q * 128 : q * 128 + 128]
        x_f[q] = x_q.reshape(HALF * OWN, 128).astype(F32)
    for n in range(6):
        table_copy(n).wait()
    top = lax.broadcasted_iota(jnp.int32, (16, 128), 0) == 0

    @pl.loop(0, OWN, unroll=8)
    def _(h):
        every = pl.ds(h, HALF, stride=OWN)
        x_h = jnp.concatenate([x_f[q, every, :] for q in range(4)], 1).astype(BF16)
        f = dot(row_fwd_ref[...], x_h)
        blocks = [(lo, lo + 16) for lo in range(0, C_ROWS, 16)]
        sides = []
        for q in range(4):
            lanes = slice(q * 128, q * 128 + 128)
            parts = []
            for lo, hi in blocks:
                co, si = cos_ref[lo:hi, lanes], sin_ref[lo:hi, lanes]
                f0, f1 = f[lo:hi, lanes], f[C_ROWS + lo : C_ROWS + hi, lanes]
                y0, y1 = f0 * co + f1 * si, f1 * co - f0 * si
                parts.append(jnp.concatenate([y0, y1], 1).astype(BF16))
            sides.append(dot(jnp.concatenate(parts, 0), fwd_ref[q]))

        parts = [[] for _ in range(4)]
        for lo, hi in blocks:
            re = [sides[q][lo:hi, 0:128] for q in range(4)]
            im = [sides[q][lo:hi, 128:256] for q in range(4)]
            t0r, t0i = re[0] + re[2], im[0] + im[2]
            t1r, t1i = re[0] - re[2], im[0] - im[2]
            t2r, t2i = re[1] + re[3], im[1] + im[3]
            t3r, t3i = re[1] - re[3], im[1] - im[3]
            zr = [t0r + t2r, t1r + t3i, t0r - t2r, t1r - t3i]
            zi = [t0i + t2i, t1i - t3r, t0i - t2i, t1i + t3r]
            pr, pi = [], []
            srows = pl.ds(h + lo * OWN, 16, stride=OWN)
            for r in range(4):
                sr, si = spec_f[0, r, srows, :], spec_f[1, r, srows, :]
                pr.append(zr[r] * sr - zi[r] * si)
                pi.append(zr[r] * si + zi[r] * sr)
            u0r, u0i = pr[0] + pr[2], pi[0] + pi[2]
            u1r, u1i = pr[0] - pr[2], pi[0] - pi[2]
            u2r, u2i = pr[1] + pr[3], pi[1] + pi[3]
            u3r, u3i = pr[1] - pr[3], pi[1] - pi[3]
            qr = [u0r + u2r, u1r - u3i, u0r - u2r, u1r + u3i]
            qi = [u0i + u2i, u1i + u3r, u0i - u2i, u1i - u3r]
            for q in range(4):
                parts[q].append(jnp.concatenate([qr[q], qi[q]], 1).astype(BF16))

        columns = []
        for q in range(4):
            lanes = slice(q * 128, q * 128 + 128)
            back = dot(jnp.concatenate(parts[q], 0), inv_ref[q])
            v0, v1 = [], []
            for lo, hi in blocks:
                co, si = cos_ref[lo:hi, lanes], sin_ref[lo:hi, lanes]
                b0, b1 = back[lo:hi, 0:128], back[lo:hi, 128:256]
                v0.append(b0 * co - b1 * si)
                v1.append(b1 * co + b0 * si)
            v1[0] = jnp.where(top, v0[8], v1[0])
            columns.append(jnp.concatenate([v.astype(BF16) for v in v0[:8] + v1[:8]], 0))
        conv = dot(row_inv_ref[...], jnp.concatenate(columns, 1)) * (1.0 / SPAN)
        for q in range(4):
            conv_f[q, every, :] = conv[:, q * 128 : q * 128 + 128]

    skip = skip_ref[...].reshape(1, OWN, 1)
    left = lax.broadcasted_iota(jnp.int32, (16, OWN, 128), 2) < 64

    @pl.loop(0, 8, unroll=8)
    def _(part):
        a0 = pl.multiple_of(part * 16, 16)
        kept = []
        for q in range(4):
            conv = conv_f[q, pl.ds(a0 * OWN, 16 * OWN), :].astype(BF16).astype(F32)
            x_q = x_f[q, pl.ds(a0 * OWN, 16 * OWN), :]
            kept.append(conv.reshape(16, OWN, 128) + skip * x_q.reshape(16, OWN, 128))
        low, high = [], []
        for n in range(2):
            even, odd = kept[2 * n], kept[2 * n + 1]
            low.append(jnp.where(left, even, pltpu.roll(odd, 64, 2)))
            high.append(jnp.where(left, pltpu.roll(even, 64, 2), odd))
        out_ref[pl.ds(a0, 16), 0] = jnp.concatenate(low, 1).astype(BF16)
        out_ref[pl.ds(a0, 16), 1] = jnp.concatenate(high, 1).astype(BF16)


def in_vmem(value):
    return pltpu.with_memory_space_constraint(value, pltpu.VMEM)


def convolve(msg, skip, tb):
    vmem = pl.BlockSpec(memory_space=pltpu.VMEM)
    hbm = pl.BlockSpec(memory_space=pltpu.HBM)
    tabs = [jnp.asarray(tb[n]) for n in TABLES]
    return pl.pallas_call(
        conv_kernel,
        in_specs=[hbm, vmem] + [hbm] * len(tabs),
        out_specs=vmem,
        out_shape=jax.ShapeDtypeStruct((HALF, 2, 16, 128), BF16),
        scratch_shapes=[
            pltpu.VMEM((SEQ, S_ROWS + X_ROWS, COLS), BF16),
            *(pltpu.VMEM(t.shape, t.dtype) for t in tabs),
            pltpu.VMEM((4, HALF * OWN, 128), F32),
            pltpu.VMEM((2, 4, HALF * OWN + OWN, 128), F32),
            pltpu.VMEM((2, 4, C_ROWS * OWN, 128), F32),
            pltpu.VMEM((4, HALF * OWN, 128), F32),
            pltpu.SemaphoreType.DMA((9,)),
            pltpu.SemaphoreType.DMA((7,)),
        ],
        compiler_params=pltpu.CompilerParams(vmem_limit_bytes=40 * 1024 * 1024),
        name="convolve",
    )(msg, in_vmem(skip), *tabs)


def mlp_kernel(place_ref, x_ref, unperm_ref, *refs):
    held = refs[0:4], refs[4:8]
    out_ref, w_ref, stream_s, gate_s, up_s, down_s, gain_s, sem = refs[8:]
    y, x, core = place_ref[0], place_ref[1], place_ref[2]

    def block_of(n):
        return lax.rem(y + lax.rem(n, 2), 2) * 4 + lax.rem(x - n // 2 + 4, 4)

    def copies(part, k):
        rows = (pl.ds(1536, W_ROWS - 1536), pl.ds(0, 1536))[part]
        for twin in range(2):
            half = lax.rem(core + twin, 2)
            yield pltpu.make_async_copy(
                held[twin][k].at[:, rows, :],
                w_ref.at[pl.ds(2 * k, 2), half, rows, :],
                sem.at[part, k, twin],
            )

    for part in range(2):
        for k in range(4):
            for copy in copies(part, k):
                copy.start()

    total = jnp.zeros((1, TOK), F32)
    for i in range(8):
        rows = x_ref[:, i].astype(F32)
        rows = jnp.concatenate([rows[:, 0:8, :], rows[:, 8:16, :]], 2).reshape(WIDTH, TOK)
        stream_s[i] = rows
        total = total + jnp.sum(rows * rows, axis=0, keepdims=True)
    scale = lax.rsqrt(total * (1.0 / D) + 1e-05)
    for k in range(4):
        for copy in copies(0, k):
            copy.wait()
    parts = jnp.concatenate([w_ref[n, 0, 1920:1936, :] for n in range(8)], 1)
    gain_s[...] = lax.dot_general(
        parts, jnp.ones((16, 128), BF16), (((0,), (0,)), ((), ())), preferred_element_type=F32
    )

    for n in range(8):
        i = block_of(n)
        gain = gain_s[n * WIDTH : n * WIDTH + WIDTH, :]
        normed = (stream_s[i] * scale * jnp.concatenate([gain, gain], 1)).astype(BF16)
        rows = pl.ds(pl.multiple_of(i * PIECE, PIECE), PIECE)
        for half in range(2):
            mid = dot(w_ref[n, half, 1536:1792, :], normed).astype(BF16)
            for m in range(4):
                gate_s[half * 4 + m, rows, :] = mid[m * PIECE : m * PIECE + PIECE]
                m1 = 128 + m * PIECE
                up_s[half * 4 + m, rows, :] = mid[m1 : m1 + PIECE]

    def block(n):
        j = block_of(n)
        gate_in, up_in = gate_s[j], up_s[j]
        acts, lefts = [], []
        for half in range(2):
            for m in range(2):
                r0 = m * 256
                gate = dot(w_ref[n, half, r0 : r0 + 256, :], gate_in)
                upper = dot(w_ref[n, half, 512 + r0 : 768 + r0, :], up_in)
                acts.append((jax.nn.gelu(gate, approximate=True) * upper).astype(BF16))
                lefts.append(w_ref[n, half, 1024 + r0 : 1280 + r0, :])
        mid = dot(jnp.concatenate(lefts, 1), jnp.concatenate(acts, 0)).astype(BF16)
        rows = pl.ds(pl.multiple_of(j * PIECE, PIECE), PIECE)
        for o in range(8):
            down_s[o, rows, :] = mid[o * PIECE : o * PIECE + PIECE]

    for group in range(2):
        for k in range(2):
            for copy in copies(1, group * 2 + k):
                copy.wait()
        for n in range(4):
            block(group * 4 + n)

    unperm = unperm_ref[...]
    for n in range(8):
        o = block_of(n)
        down = down_s[o]
        res = jnp.concatenate([dot(w_ref[n, half, 1792:1920, :], down) for half in range(2)], 0)
        res = (stream_s[o] + res).astype(BF16)
        out_ref[o] = dot_nt(unperm, res).astype(BF16)


def mlp(place, x, held, twins, tb):
    vmem = pl.BlockSpec(memory_space=pltpu.VMEM)
    hbm = pl.BlockSpec(memory_space=pltpu.HBM)
    return pl.pallas_call(
        mlp_kernel,
        in_specs=[pl.BlockSpec(memory_space=pltpu.SMEM), vmem, vmem] + [hbm] * 8,
        out_specs=vmem,
        out_shape=jax.ShapeDtypeStruct((8, TOK, WIDTH), BF16),
        scratch_shapes=[
            pltpu.VMEM((8, 2, W_ROWS, PB), BF16),
            pltpu.VMEM((8, WIDTH, TOK), F32),
            pltpu.VMEM((8, PB, TOK), BF16),
            pltpu.VMEM((8, PB, TOK), BF16),
            pltpu.VMEM((8, PB, TOK), BF16),
            pltpu.VMEM((D, 128), F32),
            pltpu.SemaphoreType.DMA((2, 4, 2)),
        ],
        compiler_params=pltpu.CompilerParams(vmem_limit_bytes=40 * 1024 * 1024),
        name="mlp",
    )(place, in_vmem(x), in_vmem(jnp.asarray(tb["unperm"])), *held, *twins)


def exchange(value, axis):
    return lax.all_to_all(value, axis, split_axis=0, concat_axis=0, tiled=True)


SEQ_AXES = ("chip", "core")


def per_device(
    tokens, spectrum, skip_gain, norm_gain,
    gate_first, up_first, gate_second, up_second, down_first, down_second,
):
    tb = tables()
    core = lax.axis_index("core").astype(jnp.int32).reshape(1)
    raw = (gate_first, up_first, gate_second, up_second, down_first, down_second)
    msg, weights = pack(tokens, spectrum, core, raw, norm_gain.reshape(1, WIDTH), tb)
    other = lax.ppermute(weights, "chan", [(n, n ^ 4) for n in range(CHAN)])
    pair = jnp.stack([weights, other])
    held = [pair]
    for k in range(1, 4):
        held.append(lax.ppermute(pair, "chan", [(n, n // 4 * 4 + (n + k) % 4) for n in range(CHAN)]))
    twins = [lax.ppermute(part, "core", [(0, 1), (1, 0)]) for part in held]
    skip = lax.dynamic_slice(skip_gain, (lax.axis_index(SEQ_AXES) * OWN,), (OWN,)).reshape(OWN, 1)
    stream = convolve(exchange(msg, SEQ_AXES), skip, tb).reshape(SEQ * CHAN, 16, 128)
    stream = exchange(stream, SEQ_AXES + ("chan",)).reshape(SEQ, CHAN, 16, 128)
    chan = lax.axis_index("chan")
    place = jnp.stack([chan // 4, chan % 4, lax.axis_index("core")]).astype(jnp.int32)
    out = mlp(place, stream, held, twins, tb)
    return exchange(out, "chan").reshape(ROWS_DEV * COLS, WIDTH)


def solution(mesh):
    split = jax.sharding.Mesh(mesh.devices.reshape(SEQ // 2, 2, CHAN), ("chip", "core", "chan"))
    in_specs = (
        P(SEQ_AXES, "chan"),
        P(None, SEQ_AXES, None, "chan"),
        P("chan"),
        P("chan"),
        P("chan", None, None),
        P("chan", None, None),
        P("chan", None, None),
        P("chan", None, None),
        P("chan", None, None),
        P("chan", None, None),
    )
    return jax.shard_map(
        per_device, mesh=split, in_specs=in_specs, out_specs=P(SEQ_AXES, "chan"), check_vma=False
    )
```

```python
import functools

import jax
import jax.numpy as jnp
import ml_dtypes
import numpy as np
from jax import lax
from jax.experimental import pallas as pl
from jax.experimental.pallas import tpu as pltpu
from jax.sharding import PartitionSpec as P

D = 2048
COLS = 512
AROWS = 256
SPAN = 131072
SEQ = 32
CHAN = 8
OWN = 8
WIDTH = 256
PB = 256
HB = 1024
PIECE = 32
ROWS_DEV = 4
TOK = 256
S_ROWS = 128
X_ROWS = 32
F32 = jnp.float32
BF16 = jnp.bfloat16
VMEM_LIMIT = 56 * 1024 * 1024


def bf16(values):
    return np.asarray(values, np.float64).astype(np.float32).astype(ml_dtypes.bfloat16)


def angle(product, period):
    return 2.0 * np.pi / period * (product % period)


@functools.lru_cache(None)
def tables():
    cols = np.arange(COLS)
    perm_cols = (cols % 128) * 4 + cols // 128
    perm = np.zeros((COLS, COLS))
    perm[cols, perm_cols] = 1.0
    place = np.arange(TOK)
    token = 4 * (place % 64) + 2 * (place // 128) + place // 64 % 2
    unperm = np.zeros((TOK, TOK))
    unperm[token, place] = 1.0
    half = AROWS // 2
    c = np.arange(half + 16)
    rows = angle(c[:, None] * np.arange(half)[None, :], AROWS)
    cos_a, sin_a = np.cos(rows) * (c <= half)[:, None], -np.sin(rows) * (c <= half)[:, None]
    row_fwd = np.concatenate([cos_a, sin_a], 0)
    row_inv = np.concatenate([cos_a[:half], cos_a[half : half + 1], sin_a[1:half]], 0).T
    theta = angle(c[:, None] * perm_cols[None, :], SPAN)
    fwd, inv = [], []
    for q in range(4):
        ang = angle((4 * np.arange(128) + q)[:, None] * np.arange(128)[None, :], COLS)
        co, si = np.cos(ang), np.sin(ang)
        fwd.append(np.block([[co, -si], [si, co]]))
        inv.append(np.block([[co.T, si.T], [-si.T, co.T]]))
    return dict(
        perm=bf16(perm),
        unperm=bf16(unperm),
        row_fwd=bf16(row_fwd),
        row_inv=bf16(row_inv),
        cos=np.cos(theta).astype(np.float32),
        sin=np.sin(theta).astype(np.float32),
        flip=bf16(np.eye(256)[::-1]),
        fwd=bf16(np.stack(fwd)),
        inv=bf16(np.stack(inv)),
    )


def dot(a, b):
    return jnp.dot(a, b, preferred_element_type=F32)


def dot_nt(a, b):
    return lax.dot_general(a, b, (((1,), (1,)), ((), ())), preferred_element_type=F32)


def params():
    return pltpu.CompilerParams(vmem_limit_bytes=VMEM_LIMIT)


W_ROWS = 1936
PIECES = 4


def pack_kernel(core_ref, tok_hbm, spec_hbm, perm_hbm, *refs):
    weights_hbm, (msg_ref, w_ref), refs = refs[:7], refs[7:9], refs[9:]
    tok_s, spec_s, perm_s, g1_s, u1_s, g2_s, u2_s, d1_s, d2_s, gain_s, msg_s, w_s = refs[:12]
    in_sem, w_sem, out_sem = refs[12:]
    core = core_ref[0]

    def columns(n):
        return pl.ds(pl.multiple_of(core * n, n), n)

    def fetch(source, target, sem):
        return pltpu.make_async_copy(source, target, sem)

    def spec_fetch(n):
        return fetch(spec_hbm.at[pl.ds(4 * n, 4)], spec_s.at[pl.ds(4 * n, 4)], in_sem.at[n])

    raw = [
        fetch(ref.at[0, :, columns(target.shape[1])], target, w_sem.at[n])
        for n, (ref, target) in enumerate(zip(weights_hbm[:4], (g1_s, u1_s, g2_s, u2_s)))
    ]
    raw.append(fetch(weights_hbm[4].at[0, columns(512), :], d1_s, w_sem.at[4]))
    raw.append(fetch(weights_hbm[5].at[0, :, columns(128)], d2_s, w_sem.at[5]))
    raw.append(fetch(weights_hbm[6], gain_s, w_sem.at[6]))
    tokens = [fetch(tok_hbm, tok_s, in_sem.at[4]), fetch(perm_hbm, perm_s, in_sem.at[5])]
    for n in range(4):
        spec_fetch(n).start()
    for copy in raw + tokens:
        copy.start()

    def turned(tiles):
        tiles = [tile.T.astype(F32).reshape(SEQ, OWN, COLS) for tile in tiles]
        return jnp.concatenate(tiles, 1).astype(BF16)

    sent = []

    def send(rows, at):
        for n in range(PIECES):
            part = pl.ds(n * (SEQ // PIECES), SEQ // PIECES)
            copy = pltpu.make_async_copy(
                msg_s.at[part, rows, :], msg_ref.at[part, rows, :], out_sem.at[at, n]
            )
            copy.start()
            sent.append(copy)

    for n in range(4):
        spec_fetch(n).wait()
        for m in range(2):
            pair = turned([spec_s[4 * n + 2 * m], spec_s[4 * n + 2 * m + 1]])
            msg_s[:, n * 32 + m * 16 : n * 32 + m * 16 + 16, :] = pair
        send(pl.ds(n * 32, 32), n)

    for copy in raw:
        copy.wait()
    tiles = [g2_s[:, 0:256], g2_s[:, 256:512], u2_s[:, 0:256], u2_s[:, 256:512]]
    tiles += [d1_s[0:256, :], d1_s[256:512, :]]
    for n, tile in enumerate(tiles):
        w_s[n * 256 : n * 256 + 256, :] = tile.T
    for n, ref in enumerate((g1_s, u1_s, d2_s)):
        r0 = 1536 + n * 128
        w_s[r0 : r0 + 128, :] = ref[...].T
    gain = gain_s[...]
    high = gain.astype(BF16).astype(F32)
    mid = (gain - high).astype(BF16).astype(F32)
    low = gain - high - mid
    w_s[1920:, :] = jnp.concatenate([high, mid, low, jnp.zeros((13, PB), F32)], 0).astype(BF16)
    w_copy = pltpu.make_async_copy(w_s, w_ref, w_sem.at[7])
    w_copy.start()
    sent.append(w_copy)

    for copy in tokens:
        copy.wait()
    perm = perm_s[...]
    for m in range(2):
        pair = [dot(perm, tok_s[2 * m + n]).astype(BF16) for n in range(2)]
        msg_s[:, S_ROWS + m * 16 : S_ROWS + m * 16 + 16, :] = turned(pair)
    send(pl.ds(S_ROWS, X_ROWS), 4)
    for copy in sent:
        copy.wait()


def pack(tokens, spectrum, core, weights, gain, tb):
    tok = tokens.reshape(ROWS_DEV, COLS, WIDTH)
    spec = spectrum.reshape(16, COLS, WIDTH)
    hbm = pl.BlockSpec(memory_space=pltpu.HBM)
    shapes = [tok.shape, spec.shape, (COLS, COLS), (PB, 128), (PB, 128), (PB, 512), (PB, 512)]
    shapes += [(512, PB), (PB, 128)]
    return pl.pallas_call(
        pack_kernel,
        in_specs=[pl.BlockSpec(memory_space=pltpu.SMEM)] + [hbm] * 10,
        out_specs=[hbm, hbm],
        out_shape=[
            jax.ShapeDtypeStruct((SEQ, S_ROWS + X_ROWS, COLS), BF16),
            jax.ShapeDtypeStruct((W_ROWS, PB), BF16),
        ],
        scratch_shapes=[
            *(pltpu.VMEM(shape, BF16) for shape in shapes),
            pltpu.VMEM((1, WIDTH), F32),
            pltpu.VMEM((SEQ, S_ROWS + X_ROWS, COLS), BF16),
            pltpu.VMEM((W_ROWS, PB), BF16),
            pltpu.SemaphoreType.DMA((6,)),
            pltpu.SemaphoreType.DMA((8,)),
            pltpu.SemaphoreType.DMA((5, PIECES)),
        ],
        compiler_params=params(),
        name="pack",
    )(core, tok, spec, jnp.asarray(tb["perm"]), *weights, gain)


HALF = AROWS // 2
C_ROWS = HALF + 16
MIRROR = SEQ // 2
TABLES = ("row_fwd", "row_inv", "cos", "sin", "fwd", "inv", "flip")


def conv_kernel(msg_hbm, skip_ref, *refs):
    tables_hbm, out_ref, msg_ref = refs[:7], refs[7], refs[8]
    table_refs, (x_f, flip_f, spec_f, conv_f, sem, table_sem) = refs[9:16], refs[16:]
    row_fwd_ref, row_inv_ref, cos_ref, sin_ref, fwd_ref, inv_ref, flip_ref = table_refs

    def spec_copy(part):
        devs, rows = pl.ds(part * 4, 4), pl.ds(0, S_ROWS)
        return pltpu.make_async_copy(msg_hbm.at[devs, rows, :], msg_ref.at[devs, rows, :], sem.at[part])

    def table_copy(n):
        return pltpu.make_async_copy(tables_hbm[n], table_refs[n], table_sem.at[n])

    rows = pl.ds(S_ROWS, X_ROWS)
    x_copy = pltpu.make_async_copy(msg_hbm.at[:, rows, :], msg_ref.at[:, rows, :], sem.at[8])
    table_copy(6).start()
    for part in range(4, 8):
        spec_copy(part).start()
    for part in range(4):
        spec_copy(part).start()
    x_copy.start()
    for n in range(6):
        table_copy(n).start()

    flip_f[:, :, HALF * OWN :, :] = jnp.zeros((2, 4, OWN, 128), F32)
    spec_f[:, :, HALF * OWN :, :] = jnp.zeros((2, 4, 16 * OWN, 128), F32)
    table_copy(6).wait()
    flip = flip_ref[...]
    for part in range(4):
        spec_copy(part + 4).wait()
        for k in range(2):
            for pair in range(2):
                lanes = slice(pair * 256, pair * 256 + 256)
                block = msg_ref[MIRROR + part * 4 : MIRROR + part * 4 + 4, k * 64 : k * 64 + 64, lanes]
                turned = dot(block.reshape(256, 256), flip)
                rows = slice(part * 256, part * 256 + 256)
                flip_f[k, 2 - 2 * pair, rows, :] = turned[:, 0:128]
                flip_f[k, 3 - 2 * pair, rows, :] = turned[:, 128:256]

    for part in range(4):
        spec_copy(part).wait()

    @pl.loop(0, MIRROR, unroll=4)
    def _(dev):
        for k in range(2):
            for r in range(4):
                own = msg_ref[dev, k * 64 : k * 64 + 64, r * 128 : r * 128 + 128].astype(F32)
                mirror = [
                    flip_f[k, r, pl.ds(pl.multiple_of((HALF - j) * OWN - dev * 64, OWN), OWN), :]
                    for j in range(8)
                ]
                mirror = jnp.concatenate(mirror, 0)
                rows = pl.ds(pl.multiple_of(dev * 64, 64), 64)
                spec_f[k, r, rows, :] = own + mirror if k == 0 else own - mirror

    for k in range(2):
        for r in range(4):
            first = msg_ref[MIRROR, k * 64 : k * 64 + 16, r * 128 : r * 128 + 128].astype(F32)
            spec_f[k, r, HALF * OWN : HALF * OWN + OWN, :] = first[0:OWN]

    x_copy.wait()
    for q in range(4):
        x_q = msg_ref[:, S_ROWS:, q * 128 : q * 128 + 128]
        x_f[q] = x_q.reshape(HALF * OWN, 128).astype(F32)
    for n in range(6):
        table_copy(n).wait()
    top = lax.broadcasted_iota(jnp.int32, (16, 128), 0) == 0

    blocks = [(lo, lo + 16) for lo in range(0, C_ROWS, 16)]

    def forward(h):
        every = pl.ds(h, HALF, stride=OWN)
        x_h = jnp.concatenate([x_f[q, every, :] for q in range(4)], 1).astype(BF16)
        f = dot(row_fwd_ref[...], x_h)
        sides = []
        for q in range(4):
            lanes = slice(q * 128, q * 128 + 128)
            parts = []
            for lo, hi in blocks:
                co, si = cos_ref[lo:hi, lanes], sin_ref[lo:hi, lanes]
                f0, f1 = f[lo:hi, lanes], f[C_ROWS + lo : C_ROWS + hi, lanes]
                y0, y1 = f0 * co + f1 * si, f1 * co - f0 * si
                parts.append(jnp.concatenate([y0, y1], 1).astype(BF16))
            sides.append(dot(jnp.concatenate(parts, 0), fwd_ref[q]))
        return sides

    def middle(h, sides):
        parts = [[] for _ in range(4)]
        for lo, hi in blocks:
            re = [sides[q][lo:hi, 0:128] for q in range(4)]
            im = [sides[q][lo:hi, 128:256] for q in range(4)]
            t0r, t0i = re[0] + re[2], im[0] + im[2]
            t1r, t1i = re[0] - re[2], im[0] - im[2]
            t2r, t2i = re[1] + re[3], im[1] + im[3]
            t3r, t3i = re[1] - re[3], im[1] - im[3]
            zr = [t0r + t2r, t1r + t3i, t0r - t2r, t1r - t3i]
            zi = [t0i + t2i, t1i - t3r, t0i - t2i, t1i + t3r]
            pr, pi = [], []
            srows = pl.ds(h + lo * OWN, 16, stride=OWN)
            for r in range(4):
                sr, si = spec_f[0, r, srows, :], spec_f[1, r, srows, :]
                pr.append(zr[r] * sr - zi[r] * si)
                pi.append(zr[r] * si + zi[r] * sr)
            u0r, u0i = pr[0] + pr[2], pi[0] + pi[2]
            u1r, u1i = pr[0] - pr[2], pi[0] - pi[2]
            u2r, u2i = pr[1] + pr[3], pi[1] + pi[3]
            u3r, u3i = pr[1] - pr[3], pi[1] - pi[3]
            qr = [u0r + u2r, u1r - u3i, u0r - u2r, u1r + u3i]
            qi = [u0i + u2i, u1i + u3r, u0i - u2i, u1i - u3r]
            for q in range(4):
                parts[q].append(jnp.concatenate([qr[q], qi[q]], 1).astype(BF16))

        return [dot(jnp.concatenate(parts[q], 0), inv_ref[q]) for q in range(4)]

    def backward(h, backs):
        columns = []
        for q in range(4):
            lanes = slice(q * 128, q * 128 + 128)
            back = backs[q]
            v0, v1 = [], []
            for lo, hi in blocks:
                co, si = cos_ref[lo:hi, lanes], sin_ref[lo:hi, lanes]
                b0, b1 = back[lo:hi, 0:128], back[lo:hi, 128:256]
                v0.append(b0 * co - b1 * si)
                v1.append(b1 * co + b0 * si)
            v1[0] = jnp.where(top, v0[8], v1[0])
            columns.append(jnp.concatenate([v.astype(BF16) for v in v0[:8] + v1[:8]], 0))
        conv = dot(row_inv_ref[...], jnp.concatenate(columns, 1)) * (1.0 / SPAN)
        for q in range(4):
            conv_f[q, pl.ds(h, HALF, stride=OWN), :] = conv[:, q * 128 : q * 128 + 128]

    sides, backs = {}, {}
    for step in range(OWN + 2):
        if step < OWN:
            sides[step] = forward(step)
        if 0 <= step - 1 < OWN:
            backs[step - 1] = middle(step - 1, sides.pop(step - 1))
        if step >= 2:
            backward(step - 2, backs.pop(step - 2))

    skip = skip_ref[...].reshape(1, OWN, 1)
    left = lax.broadcasted_iota(jnp.int32, (16, OWN, 128), 2) < 64

    @pl.loop(0, 8, unroll=8)
    def _(part):
        a0 = pl.multiple_of(part * 16, 16)
        kept = []
        for q in range(4):
            conv = conv_f[q, pl.ds(a0 * OWN, 16 * OWN), :].astype(BF16).astype(F32)
            x_q = x_f[q, pl.ds(a0 * OWN, 16 * OWN), :]
            kept.append(conv.reshape(16, OWN, 128) + skip * x_q.reshape(16, OWN, 128))
        low, high = [], []
        for n in range(2):
            even, odd = kept[2 * n], kept[2 * n + 1]
            low.append(jnp.where(left, even, pltpu.roll(odd, 64, 2)))
            high.append(jnp.where(left, pltpu.roll(even, 64, 2), odd))
        out_ref[pl.ds(a0, 16), 0] = jnp.concatenate(low, 1).astype(BF16)
        out_ref[pl.ds(a0, 16), 1] = jnp.concatenate(high, 1).astype(BF16)


def in_hbm(value):
    return pltpu.with_memory_space_constraint(value, pltpu.HBM)


def in_vmem(value):
    return pltpu.with_memory_space_constraint(value, pltpu.VMEM)


def convolve(msg, skip, tb):
    vmem = pl.BlockSpec(memory_space=pltpu.VMEM)
    hbm = pl.BlockSpec(memory_space=pltpu.HBM)
    tabs = [jnp.asarray(tb[n]) for n in TABLES]
    return pl.pallas_call(
        conv_kernel,
        in_specs=[hbm, vmem] + [hbm] * len(tabs),
        out_specs=vmem,
        out_shape=jax.ShapeDtypeStruct((HALF, 2, 16, 128), BF16),
        scratch_shapes=[
            pltpu.VMEM((SEQ, S_ROWS + X_ROWS, COLS), BF16),
            *(pltpu.VMEM(t.shape, t.dtype) for t in tabs),
            pltpu.VMEM((4, HALF * OWN, 128), F32),
            pltpu.VMEM((2, 4, HALF * OWN + OWN, 128), F32),
            pltpu.VMEM((2, 4, C_ROWS * OWN, 128), F32),
            pltpu.VMEM((4, HALF * OWN, 128), F32),
            pltpu.SemaphoreType.DMA((9,)),
            pltpu.SemaphoreType.DMA((7,)),
        ],
        compiler_params=pltpu.CompilerParams(vmem_limit_bytes=40 * 1024 * 1024),
        name="convolve",
    )(msg, in_vmem(skip), *(in_hbm(t) for t in tabs))


def mlp_kernel(place_ref, x_ref, unperm_ref, *refs):
    held = refs[0:4], refs[4:8]
    out_ref, w_ref, stream_s, gate_s, up_s, down_s, gain_s, sem = refs[8:]
    y, x, core = place_ref[0], place_ref[1], place_ref[2]

    def block_of(n):
        return lax.rem(y + lax.rem(n, 2), 2) * 4 + lax.rem(x - n // 2 + 4, 4)

    def copies(part, k):
        rows = (pl.ds(1536, W_ROWS - 1536), pl.ds(0, 1536))[part]
        for twin in range(2):
            half = lax.rem(core + twin, 2)
            yield pltpu.make_async_copy(
                held[twin][k].at[:, rows, :],
                w_ref.at[pl.ds(2 * k, 2), half, rows, :],
                sem.at[part, k, twin],
            )

    for part in range(2):
        for k in range(4):
            for copy in copies(part, k):
                copy.start()

    total = jnp.zeros((1, TOK), F32)
    for i in range(8):
        rows = x_ref[:, i].astype(F32)
        rows = jnp.concatenate([rows[:, 0:8, :], rows[:, 8:16, :]], 2).reshape(WIDTH, TOK)
        stream_s[i] = rows
        total = total + jnp.sum(rows * rows, axis=0, keepdims=True)
    scale = lax.rsqrt(total * (1.0 / D) + 1e-05)
    for k in range(4):
        for copy in copies(0, k):
            copy.wait()
    parts = jnp.concatenate([w_ref[n, 0, 1920:1936, :] for n in range(8)], 1)
    gain_s[...] = lax.dot_general(
        parts, jnp.ones((16, 128), BF16), (((0,), (0,)), ((), ())), preferred_element_type=F32
    )

    for n in range(8):
        i = block_of(n)
        gain = gain_s[n * WIDTH : n * WIDTH + WIDTH, :]
        normed = (stream_s[i] * scale * jnp.concatenate([gain, gain], 1)).astype(BF16)
        rows = pl.ds(pl.multiple_of(i * PIECE, PIECE), PIECE)
        for half in range(2):
            mid = dot(w_ref[n, half, 1536:1792, :], normed).astype(BF16)
            for m in range(4):
                gate_s[half * 4 + m, rows, :] = mid[m * PIECE : m * PIECE + PIECE]
                m1 = 128 + m * PIECE
                up_s[half * 4 + m, rows, :] = mid[m1 : m1 + PIECE]

    def widen(n):
        j = block_of(n)
        gate_in, up_in = gate_s[j], up_s[j]
        halves = []
        for half in range(2):
            gate = dot(w_ref[n, half, 0:512, :], gate_in)
            halves.append((gate, dot(w_ref[n, half, 512:1024, :], up_in)))
        return halves

    def narrow(n, halves):
        j = block_of(n)
        acts, lefts = [], []
        for half, (gate, upper) in enumerate(halves):
            acts.append((jax.nn.gelu(gate, approximate=True) * upper).astype(BF16))
            for m in range(2):
                lefts.append(w_ref[n, half, 1024 + m * 256 : 1280 + m * 256, :])
        mid = dot(jnp.concatenate(lefts, 1), jnp.concatenate(acts, 0)).astype(BF16)
        rows = pl.ds(pl.multiple_of(j * PIECE, PIECE), PIECE)
        for o in range(8):
            down_s[o, rows, :] = mid[o * PIECE : o * PIECE + PIECE]

    for group in range(2):
        for k in range(2):
            for copy in copies(1, group * 2 + k):
                copy.wait()
        wide = None
        for n in range(5):
            later = widen(group * 4 + n) if n < 4 else None
            if n > 0:
                narrow(group * 4 + n - 1, wide)
            wide = later

    unperm = unperm_ref[...]
    for n in range(8):
        o = block_of(n)
        down = down_s[o]
        res = jnp.concatenate([dot(w_ref[n, half, 1792:1920, :], down) for half in range(2)], 0)
        res = (stream_s[o] + res).astype(BF16)
        out_ref[o] = dot_nt(unperm, res).astype(BF16)


def mlp(place, x, held, twins, tb):
    vmem = pl.BlockSpec(memory_space=pltpu.VMEM)
    hbm = pl.BlockSpec(memory_space=pltpu.HBM)
    return pl.pallas_call(
        mlp_kernel,
        in_specs=[pl.BlockSpec(memory_space=pltpu.SMEM), vmem, vmem] + [hbm] * 8,
        out_specs=vmem,
        out_shape=jax.ShapeDtypeStruct((8, TOK, WIDTH), BF16),
        scratch_shapes=[
            pltpu.VMEM((8, 2, W_ROWS, PB), BF16),
            pltpu.VMEM((8, WIDTH, TOK), F32),
            pltpu.VMEM((8, PB, TOK), BF16),
            pltpu.VMEM((8, PB, TOK), BF16),
            pltpu.VMEM((8, PB, TOK), BF16),
            pltpu.VMEM((D, 128), F32),
            pltpu.SemaphoreType.DMA((2, 4, 2)),
        ],
        compiler_params=pltpu.CompilerParams(vmem_limit_bytes=40 * 1024 * 1024),
        name="mlp",
    )(place, in_vmem(x), in_vmem(jnp.asarray(tb["unperm"])), *held, *twins)


def exchange(value, axis):
    return lax.all_to_all(value, axis, split_axis=0, concat_axis=0, tiled=True)


SEQ_AXES = ("chip", "core")


def per_device(
    tokens, spectrum, skip_gain, norm_gain,
    gate_first, up_first, gate_second, up_second, down_first, down_second,
):
    tb = tables()
    core = lax.axis_index("core").astype(jnp.int32).reshape(1)
    raw = (gate_first, up_first, gate_second, up_second, down_first, down_second)
    msg, weights = pack(tokens, spectrum, core, raw, norm_gain.reshape(1, WIDTH), tb)
    other = lax.ppermute(weights, "chan", [(n, n ^ 4) for n in range(CHAN)])
    pair = jnp.stack([weights, other])
    held = [pair]
    for k in range(1, 4):
        held.append(lax.ppermute(pair, "chan", [(n, n // 4 * 4 + (n + k) % 4) for n in range(CHAN)]))
    twins = [lax.ppermute(part, "core", [(0, 1), (1, 0)]) for part in held]
    skip = lax.dynamic_slice(skip_gain, (lax.axis_index(SEQ_AXES) * OWN,), (OWN,)).reshape(OWN, 1)
    stream = convolve(exchange(msg, SEQ_AXES), skip, tb).reshape(SEQ * CHAN, 16, 128)
    stream = exchange(stream, SEQ_AXES + ("chan",)).reshape(SEQ, CHAN, 16, 128)
    chan = lax.axis_index("chan")
    place = jnp.stack([chan // 4, chan % 4, lax.axis_index("core")]).astype(jnp.int32)
    out = mlp(place, stream, held, twins, tb)
    return exchange(out, "chan").reshape(ROWS_DEV * COLS, WIDTH)


def solution(mesh):
    split = jax.sharding.Mesh(mesh.devices.reshape(SEQ // 2, 2, CHAN), ("chip", "core", "chan"))
    in_specs = (
        P(SEQ_AXES, "chan"),
        P(None, SEQ_AXES, None, "chan"),
        P("chan"),
        P("chan"),
        P("chan", None, None),
        P("chan", None, None),
        P("chan", None, None),
        P("chan", None, None),
        P("chan", None, None),
        P("chan", None, None),
    )
    return jax.shard_map(
        per_device, mesh=split, in_specs=in_specs, out_specs=P(SEQ_AXES, "chan"), check_vma=False
    )
```

```python
import functools

import jax
import jax.numpy as jnp
import ml_dtypes
import numpy as np
from jax import lax
from jax.experimental import pallas as pl
from jax.experimental.pallas import tpu as pltpu
from jax.sharding import PartitionSpec as P

D = 2048
COLS = 512
AROWS = 256
SPAN = 131072
SEQ = 32
CHAN = 8
OWN = 8
WIDTH = 256
PB = 256
HB = 1024
PIECE = 32
ROWS_DEV = 4
TOK = 256
S_ROWS = 128
X_ROWS = 32
F32 = jnp.float32
BF16 = jnp.bfloat16
VMEM_LIMIT = 56 * 1024 * 1024


def bf16(values):
    return np.asarray(values, np.float64).astype(np.float32).astype(ml_dtypes.bfloat16)


def angle(product, period):
    return 2.0 * np.pi / period * (product % period)


@functools.lru_cache(None)
def tables():
    cols = np.arange(COLS)
    perm_cols = (cols % 128) * 4 + cols // 128
    perm = np.zeros((COLS, COLS))
    perm[cols, perm_cols] = 1.0
    place = np.arange(TOK)
    token = 4 * (place % 64) + 2 * (place // 128) + place // 64 % 2
    unperm = np.zeros((TOK, TOK))
    unperm[token, place] = 1.0
    half = AROWS // 2
    c = np.arange(half + 16)
    rows = angle(c[:, None] * np.arange(half)[None, :], AROWS)
    cos_a, sin_a = np.cos(rows) * (c <= half)[:, None], -np.sin(rows) * (c <= half)[:, None]
    row_fwd = np.concatenate([cos_a, sin_a], 0)
    row_inv = np.concatenate([cos_a[:half], cos_a[half : half + 1], sin_a[1:half]], 0).T
    theta = angle(c[:, None] * perm_cols[None, :], SPAN)
    fwd, inv = [], []
    for q in range(4):
        ang = angle((4 * np.arange(128) + q)[:, None] * np.arange(128)[None, :], COLS)
        co, si = np.cos(ang), np.sin(ang)
        fwd.append(np.block([[co, -si], [si, co]]))
        inv.append(np.block([[co.T, si.T], [-si.T, co.T]]))
    return dict(
        perm=bf16(perm),
        unperm=bf16(unperm),
        row_fwd=bf16(row_fwd),
        row_inv=bf16(row_inv),
        cos=np.cos(theta).astype(np.float32),
        sin=np.sin(theta).astype(np.float32),
        flip=bf16(np.eye(256)[::-1]),
        fwd=bf16(np.stack(fwd)),
        inv=bf16(np.stack(inv)),
    )


def dot(a, b):
    return jnp.dot(a, b, preferred_element_type=F32)


def dot_nt(a, b):
    return lax.dot_general(a, b, (((1,), (1,)), ((), ())), preferred_element_type=F32)


def params():
    return pltpu.CompilerParams(vmem_limit_bytes=VMEM_LIMIT)


W_ROWS = 1936
PIECES = 4


def pack_kernel(core_ref, tok_hbm, spec_hbm, perm_hbm, *refs):
    weights_hbm, (msg_ref, w_ref), refs = refs[:7], refs[7:9], refs[9:]
    tok_s, spec_s, perm_s, g1_s, u1_s, g2_s, u2_s, d1_s, d2_s, gain_s, msg_s, w_s = refs[:12]
    in_sem, w_sem, out_sem = refs[12:]
    core = core_ref[0]

    def columns(n):
        return pl.ds(pl.multiple_of(core * n, n), n)

    def fetch(source, target, sem):
        return pltpu.make_async_copy(source, target, sem)

    def spec_fetch(n):
        return fetch(spec_hbm.at[pl.ds(4 * n, 4)], spec_s.at[pl.ds(4 * n, 4)], in_sem.at[n])

    raw = [
        fetch(ref.at[0, :, columns(target.shape[1])], target, w_sem.at[n])
        for n, (ref, target) in enumerate(zip(weights_hbm[:4], (g1_s, u1_s, g2_s, u2_s)))
    ]
    raw.append(fetch(weights_hbm[4].at[0, columns(512), :], d1_s, w_sem.at[4]))
    raw.append(fetch(weights_hbm[5].at[0, :, columns(128)], d2_s, w_sem.at[5]))
    raw.append(fetch(weights_hbm[6], gain_s, w_sem.at[6]))
    tokens = [fetch(tok_hbm, tok_s, in_sem.at[4]), fetch(perm_hbm, perm_s, in_sem.at[5])]
    for n in range(4):
        spec_fetch(n).start()
    for copy in raw + tokens:
        copy.start()

    def turned(tiles):
        tiles = [tile.T.astype(F32).reshape(SEQ, OWN, COLS) for tile in tiles]
        return jnp.concatenate(tiles, 1).astype(BF16)

    sent = []

    def send(rows, at):
        for n in range(PIECES):
            part = pl.ds(n * (SEQ // PIECES), SEQ // PIECES)
            copy = pltpu.make_async_copy(
                msg_s.at[part, rows, :], msg_ref.at[part, rows, :], out_sem.at[at, n]
            )
            copy.start()
            sent.append(copy)

    for n in range(4):
        spec_fetch(n).wait()
        for m in range(2):
            pair = turned([spec_s[4 * n + 2 * m], spec_s[4 * n + 2 * m + 1]])
            msg_s[:, n * 32 + m * 16 : n * 32 + m * 16 + 16, :] = pair
        send(pl.ds(n * 32, 32), n)

    for copy in raw:
        copy.wait()
    tiles = [g2_s[:, 0:256], g2_s[:, 256:512], u2_s[:, 0:256], u2_s[:, 256:512]]
    tiles += [d1_s[0:256, :], d1_s[256:512, :]]
    for n, tile in enumerate(tiles):
        w_s[n * 256 : n * 256 + 256, :] = tile.T
    for n, ref in enumerate((g1_s, u1_s, d2_s)):
        r0 = 1536 + n * 128
        w_s[r0 : r0 + 128, :] = ref[...].T
    gain = gain_s[...]
    high = gain.astype(BF16).astype(F32)
    mid = (gain - high).astype(BF16).astype(F32)
    low = gain - high - mid
    w_s[1920:, :] = jnp.concatenate([high, mid, low, jnp.zeros((13, PB), F32)], 0).astype(BF16)
    w_copy = pltpu.make_async_copy(w_s, w_ref, w_sem.at[7])
    w_copy.start()
    sent.append(w_copy)

    for copy in tokens:
        copy.wait()
    perm = perm_s[...]
    for m in range(2):
        pair = [dot(perm, tok_s[2 * m + n]).astype(BF16) for n in range(2)]
        msg_s[:, S_ROWS + m * 16 : S_ROWS + m * 16 + 16, :] = turned(pair)
    send(pl.ds(S_ROWS, X_ROWS), 4)
    for copy in sent:
        copy.wait()


def pack(tokens, spectrum, core, weights, gain, tb):
    tok = tokens.reshape(ROWS_DEV, COLS, WIDTH)
    spec = spectrum.reshape(16, COLS, WIDTH)
    hbm = pl.BlockSpec(memory_space=pltpu.HBM)
    shapes = [tok.shape, spec.shape, (COLS, COLS), (PB, 128), (PB, 128), (PB, 512), (PB, 512)]
    shapes += [(512, PB), (PB, 128)]
    return pl.pallas_call(
        pack_kernel,
        in_specs=[pl.BlockSpec(memory_space=pltpu.SMEM)] + [hbm] * 10,
        out_specs=[hbm, hbm],
        out_shape=[
            jax.ShapeDtypeStruct((SEQ, S_ROWS + X_ROWS, COLS), BF16),
            jax.ShapeDtypeStruct((W_ROWS, PB), BF16),
        ],
        scratch_shapes=[
            *(pltpu.VMEM(shape, BF16) for shape in shapes),
            pltpu.VMEM((1, WIDTH), F32),
            pltpu.VMEM((SEQ, S_ROWS + X_ROWS, COLS), BF16),
            pltpu.VMEM((W_ROWS, PB), BF16),
            pltpu.SemaphoreType.DMA((6,)),
            pltpu.SemaphoreType.DMA((8,)),
            pltpu.SemaphoreType.DMA((5, PIECES)),
        ],
        compiler_params=params(),
        name="pack",
    )(core, tok, spec, jnp.asarray(tb["perm"]), *weights, gain)


HALF = AROWS // 2
C_ROWS = HALF + 16
MIRROR = SEQ // 2
TABLES = ("row_fwd", "row_inv", "cos", "sin", "fwd", "inv", "flip")


def conv_kernel(msg_hbm, skip_ref, *refs):
    tables_hbm, out_ref, msg_ref = refs[:7], refs[7], refs[8]
    table_refs, (x_f, flip_f, spec_f, conv_f, sem, table_sem) = refs[9:16], refs[16:]
    row_fwd_ref, row_inv_ref, cos_ref, sin_ref, fwd_ref, inv_ref, flip_ref = table_refs

    def spec_copy(part):
        devs, rows = pl.ds(part * 4, 4), pl.ds(0, S_ROWS)
        return pltpu.make_async_copy(msg_hbm.at[devs, rows, :], msg_ref.at[devs, rows, :], sem.at[part])

    def table_copy(n):
        return pltpu.make_async_copy(tables_hbm[n], table_refs[n], table_sem.at[n])

    rows = pl.ds(S_ROWS, X_ROWS)
    x_copy = pltpu.make_async_copy(msg_hbm.at[:, rows, :], msg_ref.at[:, rows, :], sem.at[8])
    table_copy(6).start()
    for part in range(4, 8):
        spec_copy(part).start()
    for part in range(4):
        spec_copy(part).start()
    x_copy.start()
    for n in range(6):
        table_copy(n).start()

    flip_f[:, :, HALF * OWN :, :] = jnp.zeros((2, 4, OWN, 128), F32)
    spec_f[:, :, HALF * OWN : C_ROWS * OWN, :] = jnp.zeros((2, 4, 16 * OWN, 128), F32)
    table_copy(6).wait()
    flip = flip_ref[...]
    for part in range(4):
        spec_copy(part + 4).wait()
        for k in range(2):
            for pair in range(2):
                lanes = slice(pair * 256, pair * 256 + 256)
                block = msg_ref[MIRROR + part * 4 : MIRROR + part * 4 + 4, k * 64 : k * 64 + 64, lanes]
                turned = dot(block.reshape(256, 256), flip)
                rows = slice(part * 256, part * 256 + 256)
                flip_f[k, 2 - 2 * pair, rows, :] = turned[:, 0:128]
                flip_f[k, 3 - 2 * pair, rows, :] = turned[:, 128:256]

    for part in range(4):
        spec_copy(part).wait()

    @pl.loop(0, MIRROR, unroll=4)
    def _(dev):
        for k in range(2):
            for r in range(4):
                own = msg_ref[dev, k * 64 : k * 64 + 64, r * 128 : r * 128 + 128].astype(F32)
                mirror = [
                    flip_f[k, r, pl.ds(pl.multiple_of((HALF - j) * OWN - dev * 64, OWN), OWN), :]
                    for j in range(8)
                ]
                mirror = jnp.concatenate(mirror, 0)
                rows = pl.ds(pl.multiple_of(dev * 64, 64), 64)
                spec_f[k, r, rows, :] = own + mirror if k == 0 else own - mirror

    for k in range(2):
        for r in range(4):
            first = msg_ref[MIRROR, k * 64 : k * 64 + 16, r * 128 : r * 128 + 128].astype(F32)
            spec_f[k, r, HALF * OWN : HALF * OWN + OWN, :] = first[0:OWN]

    x_copy.wait()
    for q in range(4):
        x_q = msg_ref[:, S_ROWS:, q * 128 : q * 128 + 128]
        x_f[q, : HALF * OWN, :] = x_q.reshape(HALF * OWN, 128).astype(F32)
    for n in range(6):
        table_copy(n).wait()
    top = lax.broadcasted_iota(jnp.int32, (16, 128), 0) == 0

    blocks = [(lo, lo + 16) for lo in range(0, C_ROWS, 16)]

    def forward(h):
        every = pl.ds(h, HALF, stride=OWN)
        x_h = jnp.concatenate([x_f[q, every, :] for q in range(4)], 1).astype(BF16)
        f = dot(row_fwd_ref[...], x_h)
        sides = []
        for q in range(4):
            lanes = slice(q * 128, q * 128 + 128)
            parts = []
            for lo, hi in blocks:
                co, si = cos_ref[lo:hi, lanes], sin_ref[lo:hi, lanes]
                f0, f1 = f[lo:hi, lanes], f[C_ROWS + lo : C_ROWS + hi, lanes]
                y0, y1 = f0 * co + f1 * si, f1 * co - f0 * si
                parts.append(jnp.concatenate([y0, y1], 1).astype(BF16))
            sides.append(dot(jnp.concatenate(parts, 0), fwd_ref[q]))
        return sides

    def middle(h, sides):
        parts = [[] for _ in range(4)]
        for lo, hi in blocks:
            re = [sides[q][lo:hi, 0:128] for q in range(4)]
            im = [sides[q][lo:hi, 128:256] for q in range(4)]
            t0r, t0i = re[0] + re[2], im[0] + im[2]
            t1r, t1i = re[0] - re[2], im[0] - im[2]
            t2r, t2i = re[1] + re[3], im[1] + im[3]
            t3r, t3i = re[1] - re[3], im[1] - im[3]
            zr = [t0r + t2r, t1r + t3i, t0r - t2r, t1r - t3i]
            zi = [t0i + t2i, t1i - t3r, t0i - t2i, t1i + t3r]
            pr, pi = [], []
            srows = pl.ds(h + lo * OWN, 16, stride=OWN)
            for r in range(4):
                sr, si = spec_f[0, r, srows, :], spec_f[1, r, srows, :]
                pr.append(zr[r] * sr - zi[r] * si)
                pi.append(zr[r] * si + zi[r] * sr)
            u0r, u0i = pr[0] + pr[2], pi[0] + pi[2]
            u1r, u1i = pr[0] - pr[2], pi[0] - pi[2]
            u2r, u2i = pr[1] + pr[3], pi[1] + pi[3]
            u3r, u3i = pr[1] - pr[3], pi[1] - pi[3]
            qr = [u0r + u2r, u1r - u3i, u0r - u2r, u1r + u3i]
            qi = [u0i + u2i, u1i + u3r, u0i - u2i, u1i - u3r]
            for q in range(4):
                parts[q].append(jnp.concatenate([qr[q], qi[q]], 1).astype(BF16))

        return [dot(jnp.concatenate(parts[q], 0), inv_ref[q]) for q in range(4)]

    def backward(h, backs):
        columns = []
        for q in range(4):
            lanes = slice(q * 128, q * 128 + 128)
            back = backs[q]
            v0, v1 = [], []
            for lo, hi in blocks:
                co, si = cos_ref[lo:hi, lanes], sin_ref[lo:hi, lanes]
                b0, b1 = back[lo:hi, 0:128], back[lo:hi, 128:256]
                v0.append(b0 * co - b1 * si)
                v1.append(b1 * co + b0 * si)
            v1[0] = jnp.where(top, v0[8], v1[0])
            columns.append(jnp.concatenate([v.astype(BF16) for v in v0[:8] + v1[:8]], 0))
        conv = dot(row_inv_ref[...], jnp.concatenate(columns, 1)) * (1.0 / SPAN)
        for q in range(4):
            conv_f[q, pl.ds(h, HALF, stride=OWN), :] = conv[:, q * 128 : q * 128 + 128]

    sides, backs = {}, {}
    for step in range(OWN + 2):
        if step < OWN:
            sides[step] = forward(step)
        if 0 <= step - 1 < OWN:
            backs[step - 1] = middle(step - 1, sides.pop(step - 1))
        if step >= 2:
            backward(step - 2, backs.pop(step - 2))

    skip = skip_ref[...].reshape(1, OWN, 1)
    left = lax.broadcasted_iota(jnp.int32, (16, OWN, 128), 2) < 64

    @pl.loop(0, 8, unroll=8)
    def _(part):
        a0 = pl.multiple_of(part * 16, 16)
        kept = []
        for q in range(4):
            conv = conv_f[q, pl.ds(a0 * OWN, 16 * OWN), :].astype(BF16).astype(F32)
            x_q = x_f[q, pl.ds(a0 * OWN, 16 * OWN), :]
            kept.append(conv.reshape(16, OWN, 128) + skip * x_q.reshape(16, OWN, 128))
        low, high = [], []
        for n in range(2):
            even, odd = kept[2 * n], kept[2 * n + 1]
            low.append(jnp.where(left, even, pltpu.roll(odd, 64, 2)))
            high.append(jnp.where(left, pltpu.roll(even, 64, 2), odd))
        out_ref[pl.ds(a0, 16), 0] = jnp.concatenate(low, 1).astype(BF16)
        out_ref[pl.ds(a0, 16), 1] = jnp.concatenate(high, 1).astype(BF16)


def in_hbm(value):
    return pltpu.with_memory_space_constraint(value, pltpu.HBM)


def in_vmem(value):
    return pltpu.with_memory_space_constraint(value, pltpu.VMEM)


def convolve(msg, skip, tb):
    vmem = pl.BlockSpec(memory_space=pltpu.VMEM)
    hbm = pl.BlockSpec(memory_space=pltpu.HBM)
    tabs = [jnp.asarray(tb[n]) for n in TABLES]
    return pl.pallas_call(
        conv_kernel,
        in_specs=[hbm, vmem] + [hbm] * len(tabs),
        out_specs=vmem,
        out_shape=jax.ShapeDtypeStruct((HALF, 2, 16, 128), BF16),
        scratch_shapes=[
            pltpu.VMEM((SEQ, S_ROWS + X_ROWS, COLS), BF16),
            *(pltpu.VMEM(t.shape, t.dtype) for t in tabs),
            pltpu.VMEM((4, HALF * OWN + OWN, 128), F32),
            pltpu.VMEM((2, 4, HALF * OWN + OWN, 128), F32),
            pltpu.VMEM((2, 4, C_ROWS * OWN + OWN, 128), F32),
            pltpu.VMEM((4, HALF * OWN + OWN, 128), F32),
            pltpu.SemaphoreType.DMA((9,)),
            pltpu.SemaphoreType.DMA((7,)),
        ],
        compiler_params=pltpu.CompilerParams(vmem_limit_bytes=40 * 1024 * 1024),
        name="convolve",
    )(msg, in_vmem(skip), *(in_hbm(t) for t in tabs))


def mlp_kernel(place_ref, x_ref, unperm_ref, *refs):
    held = refs[0:4], refs[4:8]
    out_ref, w_ref, stream_s, gate_s, up_s, down_s, gain_s, sem = refs[8:]
    y, x, core = place_ref[0], place_ref[1], place_ref[2]

    def block_of(n):
        return lax.rem(y + lax.rem(n, 2), 2) * 4 + lax.rem(x - n // 2 + 4, 4)

    def copies(part, k):
        rows = (pl.ds(1536, W_ROWS - 1536), pl.ds(0, 1536))[part]
        for twin in range(2):
            half = lax.rem(core + twin, 2)
            yield pltpu.make_async_copy(
                held[twin][k].at[:, rows, :],
                w_ref.at[pl.ds(2 * k, 2), half, rows, :],
                sem.at[part, k, twin],
            )

    for part in range(2):
        for k in range(4):
            for copy in copies(part, k):
                copy.start()

    total = jnp.zeros((1, TOK), F32)
    for i in range(8):
        rows = x_ref[:, i].astype(F32)
        rows = jnp.concatenate([rows[:, 0:8, :], rows[:, 8:16, :]], 2).reshape(WIDTH, TOK)
        stream_s[i] = rows
        total = total + jnp.sum(rows * rows, axis=0, keepdims=True)
    scale = lax.rsqrt(total * (1.0 / D) + 1e-05)
    for k in range(4):
        for copy in copies(0, k):
            copy.wait()
    parts = jnp.concatenate([w_ref[n, 0, 1920:1936, :] for n in range(8)], 1)
    gain_s[...] = lax.dot_general(
        parts, jnp.ones((16, 128), BF16), (((0,), (0,)), ((), ())), preferred_element_type=F32
    )

    for n in range(8):
        i = block_of(n)
        gain = gain_s[n * WIDTH : n * WIDTH + WIDTH, :]
        normed = (stream_s[i] * scale * jnp.concatenate([gain, gain], 1)).astype(BF16)
        rows = pl.ds(pl.multiple_of(i * PIECE, PIECE), PIECE)
        for half in range(2):
            mid = dot(w_ref[n, half, 1536:1792, :], normed).astype(BF16)
            for m in range(4):
                gate_s[half * 4 + m, rows, :] = mid[m * PIECE : m * PIECE + PIECE]
                m1 = 128 + m * PIECE
                up_s[half * 4 + m, rows, :] = mid[m1 : m1 + PIECE]

    def widen(n):
        j = block_of(n)
        gate_in, up_in = gate_s[j], up_s[j]
        halves = []
        for half in range(2):
            gate = dot(w_ref[n, half, 0:512, :], gate_in)
            halves.append((gate, dot(w_ref[n, half, 512:1024, :], up_in)))
        return halves

    def narrow(n, halves):
        j = block_of(n)
        acts, lefts = [], []
        for half, (gate, upper) in enumerate(halves):
            acts.append((jax.nn.gelu(gate, approximate=True) * upper).astype(BF16))
            for m in range(2):
                lefts.append(w_ref[n, half, 1024 + m * 256 : 1280 + m * 256, :])
        mid = dot(jnp.concatenate(lefts, 1), jnp.concatenate(acts, 0)).astype(BF16)
        rows = pl.ds(pl.multiple_of(j * PIECE, PIECE), PIECE)
        for o in range(8):
            down_s[o, rows, :] = mid[o * PIECE : o * PIECE + PIECE]

    for group in range(2):
        for k in range(2):
            for copy in copies(1, group * 2 + k):
                copy.wait()
        wide = None
        for n in range(5):
            later = widen(group * 4 + n) if n < 4 else None
            if n > 0:
                narrow(group * 4 + n - 1, wide)
            wide = later

    unperm = unperm_ref[...]
    for n in range(8):
        o = block_of(n)
        down = down_s[o]
        res = jnp.concatenate([dot(w_ref[n, half, 1792:1920, :], down) for half in range(2)], 0)
        res = (stream_s[o] + res).astype(BF16)
        out_ref[o] = dot_nt(unperm, res).astype(BF16)


def mlp(place, x, held, twins, tb):
    vmem = pl.BlockSpec(memory_space=pltpu.VMEM)
    hbm = pl.BlockSpec(memory_space=pltpu.HBM)
    return pl.pallas_call(
        mlp_kernel,
        in_specs=[pl.BlockSpec(memory_space=pltpu.SMEM), vmem, vmem] + [hbm] * 8,
        out_specs=vmem,
        out_shape=jax.ShapeDtypeStruct((8, TOK, WIDTH), BF16),
        scratch_shapes=[
            pltpu.VMEM((8, 2, W_ROWS, PB), BF16),
            pltpu.VMEM((8, WIDTH, TOK), F32),
            pltpu.VMEM((8, PB, TOK), BF16),
            pltpu.VMEM((8, PB, TOK), BF16),
            pltpu.VMEM((8, PB, TOK), BF16),
            pltpu.VMEM((D, 128), F32),
            pltpu.SemaphoreType.DMA((2, 4, 2)),
        ],
        compiler_params=pltpu.CompilerParams(vmem_limit_bytes=40 * 1024 * 1024),
        name="mlp",
    )(place, in_vmem(x), in_vmem(jnp.asarray(tb["unperm"])), *held, *twins)


def exchange(value, axis):
    return lax.all_to_all(value, axis, split_axis=0, concat_axis=0, tiled=True)


SEQ_AXES = ("chip", "core")


def per_device(
    tokens, spectrum, skip_gain, norm_gain,
    gate_first, up_first, gate_second, up_second, down_first, down_second,
):
    tb = tables()
    core = lax.axis_index("core").astype(jnp.int32).reshape(1)
    raw = (gate_first, up_first, gate_second, up_second, down_first, down_second)
    msg, weights = pack(tokens, spectrum, core, raw, norm_gain.reshape(1, WIDTH), tb)
    other = lax.ppermute(weights, "chan", [(n, n ^ 4) for n in range(CHAN)])
    pair = jnp.stack([weights, other])
    held = [pair]
    for k in range(1, 4):
        held.append(lax.ppermute(pair, "chan", [(n, n // 4 * 4 + (n + k) % 4) for n in range(CHAN)]))
    twins = [lax.ppermute(part, "core", [(0, 1), (1, 0)]) for part in held]
    skip = lax.dynamic_slice(skip_gain, (lax.axis_index(SEQ_AXES) * OWN,), (OWN,)).reshape(OWN, 1)
    stream = convolve(exchange(msg, SEQ_AXES), skip, tb).reshape(SEQ * CHAN, 16, 128)
    stream = exchange(stream, SEQ_AXES + ("chan",)).reshape(SEQ, CHAN, 16, 128)
    chan = lax.axis_index("chan")
    place = jnp.stack([chan // 4, chan % 4, lax.axis_index("core")]).astype(jnp.int32)
    out = mlp(place, stream, held, twins, tb)
    return exchange(out, "chan").reshape(ROWS_DEV * COLS, WIDTH)


def solution(mesh):
    split = jax.sharding.Mesh(mesh.devices.reshape(SEQ // 2, 2, CHAN), ("chip", "core", "chan"))
    in_specs = (
        P(SEQ_AXES, "chan"),
        P(None, SEQ_AXES, None, "chan"),
        P("chan"),
        P("chan"),
        P("chan", None, None),
        P("chan", None, None),
        P("chan", None, None),
        P("chan", None, None),
        P("chan", None, None),
        P("chan", None, None),
    )
    return jax.shard_map(
        per_device, mesh=split, in_specs=in_specs, out_specs=P(SEQ_AXES, "chan"), check_vma=False
    )
```
